32 devices in a mesh: section: 4 (over z), tower: 2 (over x), lane: 4 (over y, core).
Axes of the slice: x: 2, y: 2, z: 4, core: 2. Of those that a mesh axis runs over, the one named last changes fastest.
Arguments:
- in_flight: bfloat16 [4, 2, 64, 3072], P('section', 'tower', 'lane'), may hold values from -6 to 6
- fresh_batches: bfloat16 [4, 2, 64, 3072], P(None, 'tower', 'lane'), may hold values from -6 to 6
- offsets: int32 [4], P('lane'), may hold values from 0 to 3, as said below
- norm_gain: float32 [4, 2, 3072], P('section', 'tower'), may hold values from 0.5 to 3
- w_query: bfloat16 [4, 2, 3072, 2048], P('section', 'tower', None, 'lane'), may hold values from -0.109375 to 0.109375
- w_keyval: bfloat16 [4, 2, 2, 3072, 2048], P('section', 'tower', None, None, 'lane'), may hold values from -0.109375 to 0.109375
- w_out: bfloat16 [4, 2, 2048, 3072], P('section', 'tower', 'lane'), may hold values from -0.125 to 0.125
Outputs:
- states: bfloat16 [2, 4, 2, 64, 3072], P(None, 'section', 'tower', 'lane')
The draws below stay inside these ranges and needn't reach their ends.
Inputs may be any that keep to these rules, and one draw needn't show every extreme that they name: offsets is a permutation of 0 to 3.
All inputs are finite; a program needn't handle non-finite values.
Results may differ from the reference program's by a relative error of at most 0.017.
Values may be sent and summed in bfloat16 or wider, within the bound.
No kernel may reach another device: no remote copies, remote signals or barrier semaphores. Data moves between devices by JAX's collectives and lax.ppermute only.
A program may use at most 64 MiB of HBM per device.

```python
import jax
import jax.numpy as jnp
from jax import lax

D = 3072
HEAD_DIM = 128
HEADS = 16
TOK = 16
NF = 4
ROWS = 64
N_SECTION = 4
N_LANE = 4


def draw_offsets(key, part):
    return jax.random.permutation(key, N_LANE).astype(jnp.int32)


def draw_norm_gain(key, part):
    low, high = (jnp.log(0.5), jnp.log(2.0))
    uniform_draw = jax.random.uniform(key, (N_SECTION, 2, D), jnp.float32, low, high)
    return jnp.exp(uniform_draw).astype(jnp.float32)


def block_levels(stream_key, dims, split, low, high):
    def one(position, blocks):
        heights = jax.random.uniform(jax.random.fold_in(jax.random.fold_in(stream_key, 6), position), (blocks,), jnp.float32, low / len(split), high / len(split))
        return jnp.repeat(jnp.exp(heights), dims[position] // blocks).reshape((-1,) + (1,) * (len(dims) - position - 1))

    factor_of = one(*split[0])
    for cut in split[1:]:
        factor_of = factor_of * one(*cut)
    return factor_of


def centred(stream_key, extent, width, most, cuts=(), held_as=jnp.bfloat16):
    result = width * jax.random.normal(stream_key, extent, jnp.float32)
    if cuts:
        result = result * block_levels(stream_key, extent, cuts, -0.22, 0.18)
    return jnp.clip(result, -most, most).astype(held_as)


def setup_inputs(seed: int = 0) -> dict:
    key_list = jax.random.split(jax.random.key(seed), 8)
    in_flight = centred(key_list[0], (N_SECTION, 2, ROWS, D), 1.0, 6.0, ((0, 4), (1, 2), (2, 4)))
    fresh_batches = centred(key_list[1], (NF, 2, ROWS, D), 1.0, 6.0, ((1, 2), (2, 4)))
    offsets = draw_offsets(jax.random.fold_in(key_list[7], 71), 0)
    norm_gain = draw_norm_gain(jax.random.fold_in(key_list[7], 71), 0)
    w_query = centred(key_list[4], (N_SECTION, 2, D, HEADS * HEAD_DIM), D ** -0.5, 0.109375, ((0, 4), (1, 2), (3, 4)))
    w_keyval = centred(key_list[5], (N_SECTION, 2, 2, D, HEADS * HEAD_DIM), D ** -0.5, 0.109375, ((0, 4), (1, 2), (4, 4)))
    w_out = centred(key_list[6], (N_SECTION, 2, HEADS * HEAD_DIM, D), (HEADS * HEAD_DIM) ** -0.5, 0.125, ((0, 4), (1, 2), (2, 4)))
    return {"in_flight": in_flight, "fresh_batches": fresh_batches, "offsets": offsets, "norm_gain": norm_gain, "w_query": w_query, "w_keyval": w_keyval, "w_out": w_out}


epsilon = 1e-06

def section_layer(packed):
    state, norm_w, wq_section, wkv_section, wo_section = packed
    wide = state.astype(jnp.float32)
    normed = (wide * lax.rsqrt(lax.optimization_barrier(jnp.mean(wide * wide, -1, keepdims=True)) + epsilon) * norm_w[:, None, :]).astype(jnp.bfloat16)
    partner = normed[::-1]
    query = jnp.einsum('trd,tdh->trh', normed.astype(jnp.float32), wq_section.astype(jnp.float32)).astype(jnp.bfloat16)
    keys = jnp.einsum('trd,tdh->trh', partner.astype(jnp.float32), wkv_section[:, 0].astype(jnp.float32)).astype(jnp.bfloat16)
    values = jnp.einsum('trd,tdh->trh', partner.astype(jnp.float32), wkv_section[:, 1].astype(jnp.float32)).astype(jnp.bfloat16)
    shaped = (2, N_LANE, TOK, HEADS, HEAD_DIM)
    scores = jnp.einsum('tlqhe,tlkhe->tlhqk', query.reshape(shaped).astype(jnp.float32), keys.reshape(shaped).astype(jnp.float32)) / jnp.sqrt(jnp.float32(HEAD_DIM))
    attn_weights = jax.nn.softmax(scores, axis=-1).astype(jnp.bfloat16)
    mixed = jnp.einsum('tlhqk,tlkhe->tlqhe', attn_weights.astype(jnp.float32), values.reshape(shaped).astype(jnp.float32)).astype(jnp.bfloat16)
    head_cols = HEADS // N_LANE * HEAD_DIM
    mixed = mixed.reshape(2, ROWS, N_LANE, head_cols)
    wo_groups = wo_section.reshape(2, N_LANE, head_cols, D)
    parts = jnp.einsum('trgc,tgcd->tgrd', mixed.astype(jnp.float32), wo_groups.astype(jnp.float32))
    head_total = lax.optimization_barrier(jnp.sum(parts, axis=1))
    return (wide + head_total).astype(jnp.bfloat16)

def reference(in_flight, fresh_batches, offsets, norm_gain, w_query, w_keyval, w_out):
    first = lax.map(section_layer, (in_flight, norm_gain, w_query, w_keyval, w_out))
    shaped_fresh = fresh_batches.reshape(NF, 2, N_LANE, TOK, D)
    picked = shaped_fresh[offsets.astype(jnp.int32), :, jnp.arange(N_LANE, dtype=jnp.int32)]
    picked = jnp.transpose(picked, (1, 0, 2, 3)).reshape(2, ROWS, D)
    second_in = jnp.concatenate([picked[None], first[:-1]], axis=0)
    second = lax.map(section_layer, (second_in, norm_gain, w_query, w_keyval, w_out))
    return jnp.stack([first, second])
```

```python
import functools

import jax
import jax.numpy as jnp
from jax import lax
from jax.experimental import pallas as pl
from jax.experimental.pallas import tpu as pltpu
from jax.sharding import PartitionSpec as P

HEAD_DIM = 128
EPSILON = 1e-06
BOTH = ("tower", "lane")


def swapped(value, mask):
    count = lax.axis_size(BOTH)
    return lax.ppermute(value, BOTH, [(i, i ^ mask) for i in range(count)])


def handed_on(value):
    count = lax.axis_size("section")
    even = [(s, s ^ 1) for s in range(count) if s ^ 1 < count]
    odd = [(s, t) for s in range(1, count) for t in [((s - 1) ^ 1) + 1] if t < count]
    from_even = lax.ppermute(value, "section", even)
    from_odd = lax.ppermute(value, "section", odd) if odd else from_even
    return jnp.where(lax.axis_index("section") % 2 == 1, from_even, from_odd)


def normalized(state, gain):
    wide = state.astype(jnp.float32)
    scale = lax.rsqrt(jnp.mean(wide * wide, -1, keepdims=True) + EPSILON)
    return (wide * scale * gain[None, :]).astype(jnp.bfloat16)


def layer_kernel(tok, mine_ref, theirs_ref, wq_ref, wkv_ref, wo_ref, keep_ref, send_ref):
    half = keep_ref.shape[0]
    rows = 2 * half
    own = jnp.concatenate([mine_ref[:half], theirs_ref[:half]], 0)
    partner = jnp.concatenate([mine_ref[half:], theirs_ref[half:]], 0)

    def project(left, right):
        return jnp.dot(left, right, preferred_element_type=jnp.float32).astype(jnp.bfloat16)

    query = project(own, wq_ref[...])
    keys = project(partner, wkv_ref[0])
    values = project(partner, wkv_ref[1])
    row_clip = lax.broadcasted_iota(jnp.int32, (rows, rows), 0) // tok
    col_clip = lax.broadcasted_iota(jnp.int32, (rows, rows), 1) // tok
    same_clip = row_clip == col_clip
    mixed = []
    for start in range(0, query.shape[1], HEAD_DIM):
        head = slice(start, start + HEAD_DIM)
        scores = lax.dot_general(
            query[:, head], keys[:, head], (((1,), (1,)), ((), ())), preferred_element_type=jnp.float32
        ) * (HEAD_DIM**-0.5)
        scores = jnp.where(same_clip, scores, -jnp.inf)
        weights = jnp.exp(scores - jnp.max(scores, -1, keepdims=True))
        weights = weights / jnp.sum(weights, -1, keepdims=True)
        mixed.append(project(weights.astype(jnp.bfloat16), values[:, head]))
    part = jnp.dot(jnp.concatenate(mixed, 1), wo_ref[...], preferred_element_type=jnp.float32)
    keep_ref[...] = part[:half]
    send_ref[...] = part[half:].astype(jnp.bfloat16)


def layer_part(mine, theirs, wq, wkv, wo, tok):
    half, width = mine.shape[0] // 2, mine.shape[1]
    return pl.pallas_call(
        functools.partial(layer_kernel, tok),
        out_shape=(
            jax.ShapeDtypeStruct((half, width), jnp.float32),
            jax.ShapeDtypeStruct((half, width), jnp.bfloat16),
        ),
        in_specs=[pl.BlockSpec(memory_space=pltpu.VMEM)] * 5,
        out_specs=(pl.BlockSpec(memory_space=pltpu.VMEM),) * 2,
        compiler_params=pltpu.CompilerParams(vmem_limit_bytes=32 << 20),
    )(mine, theirs, wq, wkv, wo)


def one_tick(state, gain, wq, wkv, wo):
    tok = state.shape[0]
    lanes = lax.axis_size("lane")
    normed = normalized(state, gain)
    distances = [tower * lanes + 2 * k for tower in range(2) for k in range(lanes // 2)]
    mine = jnp.concatenate([swapped(normed, d) if d else normed for d in distances], 0)
    theirs = swapped(mine, 1)
    keep, send = layer_part(mine, theirs, wq, wkv, wo, tok)
    total = keep + swapped(send, 1).astype(jnp.float32)
    result = state.astype(jnp.float32) + total[:tok]
    for k in range(1, lanes // 2):
        share = total[k * tok : (k + 1) * tok].astype(jnp.bfloat16)
        result = result + swapped(share, 2 * k).astype(jnp.float32)
    return result.astype(jnp.bfloat16)


def shards(in_flight, fresh_batches, offsets, norm_gain, w_query, w_keyval, w_out):
    gain = norm_gain[0, 0]
    weights = (w_query[0, 0], w_keyval[0, 0], w_out[0, 0])
    picked = lax.dynamic_index_in_dim(fresh_batches[:, 0], offsets[0], 0, keepdims=False)
    first = one_tick(in_flight[0, 0], gain, *weights)
    second_in = jnp.where(lax.axis_index("section") == 0, picked, handed_on(first))
    second = one_tick(second_in, gain, *weights)
    return jnp.stack([first, second])[:, None, None]


def solution(mesh):
    placed = (
        P("section", "tower", "lane", None),
        P(None, "tower", "lane", None),
        P("lane"),
        P("section", "tower", None),
        P("section", "tower", None, "lane"),
        P("section", "tower", None, None, "lane"),
        P("section", "tower", "lane", None),
    )
    return jax.shard_map(
        shards,
        mesh=mesh,
        in_specs=placed,
        out_specs=P(None, "section", "tower", "lane", None),
        check_vma=False,
    )
```

```python
import functools
import math

import jax
import jax.numpy as jnp
from jax import lax
from jax.experimental import pallas as pl
from jax.experimental.pallas import tpu as pltpu
from jax.sharding import PartitionSpec as P

HEAD_DIM = 128
EPSILON = 1e-06
BOTH = ("tower", "lane")


def swapped(value, mask):
    count = lax.axis_size(BOTH)
    return lax.ppermute(value, BOTH, [(i, i ^ mask) for i in range(count)])


def handed_on(value):
    count = lax.axis_size("section")
    even = [(s, s ^ 1) for s in range(count) if s ^ 1 < count]
    odd = [(s, t) for s in range(1, count) for t in [((s - 1) ^ 1) + 1] if t < count]
    from_even = lax.ppermute(value, "section", even)
    from_odd = lax.ppermute(value, "section", odd) if odd else from_even
    return jnp.where(lax.axis_index("section") % 2 == 1, from_even, from_odd)


def normalized(state, gain):
    wide = state.astype(jnp.float32)
    scale = lax.rsqrt(jnp.mean(wide * wide, -1, keepdims=True) + EPSILON)
    return (wide * scale * gain).astype(jnp.bfloat16)


def layer_kernel(tok, mine_ref, theirs_ref, wq_ref, wkv_ref, wo_ref, keep_ref, send_ref):
    half = keep_ref.shape[0]
    rows = 2 * half
    own = jnp.concatenate([mine_ref[:half], theirs_ref[:half]], 0)
    partner = jnp.concatenate([mine_ref[half:], theirs_ref[half:]], 0)

    def project(left, right):
        return jnp.dot(left, right, preferred_element_type=jnp.float32).astype(jnp.bfloat16)

    query = project(own, wq_ref[...])
    keys = project(partner, wkv_ref[0])
    values = project(partner, wkv_ref[1])
    row_clip = lax.broadcasted_iota(jnp.int32, (rows, rows), 0) // tok
    col_clip = lax.broadcasted_iota(jnp.int32, (rows, rows), 1) // tok
    same_clip = row_clip == col_clip
    mixed = []
    for start in range(0, query.shape[1], HEAD_DIM):
        head = slice(start, start + HEAD_DIM)
        scores = lax.dot_general(
            query[:, head], keys[:, head], (((1,), (1,)), ((), ())), preferred_element_type=jnp.float32
        ) * (HEAD_DIM**-0.5)
        scores = jnp.where(same_clip, scores, -jnp.inf)
        weights = jnp.exp(scores - jnp.max(scores, -1, keepdims=True))
        weights = weights / jnp.sum(weights, -1, keepdims=True)
        mixed.append(project(weights.astype(jnp.bfloat16), values[:, head]))
    part = jnp.dot(jnp.concatenate(mixed, 1), wo_ref[...], preferred_element_type=jnp.float32)
    keep_ref[...] = part[:half]
    send_ref[...] = part[half:].astype(jnp.bfloat16)


def layer_part(mine, theirs, wq, wkv, wo, tok):
    half, width = mine.shape[0] // 2, mine.shape[1]
    return pl.pallas_call(
        functools.partial(layer_kernel, tok),
        out_shape=(
            jax.ShapeDtypeStruct((half, width), jnp.float32),
            jax.ShapeDtypeStruct((half, width), jnp.bfloat16),
        ),
        in_specs=[pl.BlockSpec(memory_space=pltpu.VMEM)] * 5,
        out_specs=(pl.BlockSpec(memory_space=pltpu.VMEM),) * 2,
        compiler_params=pltpu.CompilerParams(vmem_limit_bytes=16 << 20),
    )(mine, theirs, wq, wkv, wo)


def entry_kernel(x_ref, gain_ref, normed_ref, x_out, gain_out):
    normed_ref[...] = normalized(x_ref[...], gain_ref[0])
    x_out[...] = x_ref[...]
    gain_out[...] = gain_ref[...]


def entry(state, gain):
    return pl.pallas_call(
        entry_kernel,
        out_shape=(
            pltpu.VMEM(state.shape, jnp.bfloat16),
            pltpu.VMEM(state.shape, state.dtype),
            pltpu.VMEM(gain.shape, gain.dtype),
        ),
        in_specs=[pl.BlockSpec(memory_space=pltpu.VMEM)] * 2,
        out_specs=(pl.BlockSpec(memory_space=pltpu.VMEM),) * 3,
        compiler_params=pltpu.CompilerParams(vmem_limit_bytes=16 << 20),
    )(state, gain)


def load_kernel(offset_ref, fresh_ref, wq_ref, wkv_ref, wo_ref, *outs_and_sem):
    *outs, sems = outs_and_sem
    copies = [(fresh_ref.at[offset_ref[0]], outs[0])]
    for source, target in ((wq_ref, outs[1]), (wkv_ref.at[0], outs[2].at[0]), (wkv_ref.at[1], outs[2].at[1]), (wo_ref, outs[3])):
        rows = source.shape[0] // 2
        copies += [(source.at[pl.ds(i * rows, rows)], target.at[pl.ds(i * rows, rows)]) for i in range(2)]
    started = [pltpu.make_async_copy(a, b, sems.at[i]) for i, (a, b) in enumerate(copies)]
    for copy in started:
        copy.start()
    for copy in started:
        copy.wait()


def load(offsets, fresh, wq, wkv, wo):
    moved = (fresh.shape[1:], wq.shape, wkv.shape, wo.shape)
    size = 2 * sum(math.prod(shape) for shape in moved)
    return pl.pallas_call(
        load_kernel,
        out_shape=tuple(pltpu.VMEM(shape, jnp.bfloat16) for shape in moved),
        in_specs=[pl.BlockSpec(memory_space=pltpu.SMEM)] + [pl.BlockSpec(memory_space=pltpu.HBM)] * 4,
        out_specs=(pl.BlockSpec(memory_space=pltpu.VMEM),) * 4,
        scratch_shapes=[pltpu.SemaphoreType.DMA((9,))],
        cost_estimate=pl.CostEstimate(flops=0, bytes_accessed=size, transcendentals=0),
        compiler_params=pltpu.CompilerParams(vmem_limit_bytes=16 << 20),
    )(offsets, *(pltpu.with_memory_space_constraint(a, pltpu.HBM) for a in (fresh, wq, wkv, wo)))


def one_tick(state, normed, weights):
    tok = state.shape[0]
    lanes = lax.axis_size("lane")
    distances = [tower * lanes + 2 * k for tower in range(2) for k in range(lanes // 2)]
    blocks = {d: swapped(normed, d) if d else normed for d in reversed(distances)}
    mine = jnp.concatenate([blocks[d] for d in distances], 0)
    mine, weights = lax.optimization_barrier((mine, weights))
    theirs = swapped(mine, 1)
    keep, send = layer_part(mine, theirs, *weights, tok)
    total = keep + swapped(send, 1).astype(jnp.float32)
    result = state.astype(jnp.float32) + total[:tok]
    for k in range(1, lanes // 2):
        share = total[k * tok : (k + 1) * tok].astype(jnp.bfloat16)
        result = result + swapped(share, 2 * k).astype(jnp.float32)
    return result.astype(jnp.bfloat16)


def shards(in_flight, fresh_batches, offsets, norm_gain, w_query, w_keyval, w_out):
    normed, state, gain = entry(in_flight[0, 0], norm_gain[0])
    picked, *weights = load(offsets, fresh_batches[:, 0], w_query[0, 0], w_keyval[0, 0], w_out[0, 0])
    first = one_tick(state, normed, weights)
    second_in = jnp.where(lax.axis_index("section") == 0, picked, handed_on(first))
    second = one_tick(second_in, normalized(second_in, gain[0]), weights)
    return jnp.stack([first, second])[:, None, None]


def solution(mesh):
    placed = (
        P("section", "tower", "lane", None),
        P(None, "tower", "lane", None),
        P("lane"),
        P("section", "tower", None),
        P("section", "tower", None, "lane"),
        P("section", "tower", None, None, "lane"),
        P("section", "tower", "lane", None),
    )
    return jax.shard_map(
        shards,
        mesh=mesh,
        in_specs=placed,
        out_specs=P(None, "section", "tower", "lane", None),
        check_vma=False,
    )
```

```python
import functools

import jax
import jax.numpy as jnp
from jax import lax
from jax.experimental import pallas as pl
from jax.experimental.pallas import tpu as pltpu
from jax.sharding import PartitionSpec as P

HEAD_DIM = 128
EPSILON = 1e-06
BOTH = ("tower", "lane")
PIECES = 4


def swapped(value, mask):
    count = lax.axis_size(BOTH)
    return lax.ppermute(value, BOTH, [(i, i ^ mask) for i in range(count)])


def handed_on(value):
    count = lax.axis_size("section")
    return lax.ppermute(value, "section", [(s, s + 1) for s in range(count - 1)])


def in_hbm(*arrays):
    return [pltpu.with_memory_space_constraint(a, pltpu.HBM) for a in arrays]


def normalized(state, gain):
    wide = state.astype(jnp.float32)
    scale = lax.rsqrt(jnp.mean(wide * wide, -1, keepdims=True) + EPSILON)
    return (wide * scale * gain).astype(jnp.bfloat16)


def layer_kernel(tok, mine_ref, theirs_ref, wq_ref, wkv_ref, wo_ref, keep_ref, send_ref):
    half, depth = keep_ref.shape
    rows = 2 * half
    own = jnp.concatenate([mine_ref[:half], theirs_ref[:half]], 0)
    partner = jnp.concatenate([mine_ref[half:], theirs_ref[half:]], 0)

    def project(left, right):
        return jnp.dot(left, right, preferred_element_type=jnp.float32).astype(jnp.bfloat16)

    query = project(own, wq_ref[...])
    keys = project(partner, wkv_ref[:depth])
    values = project(partner, wkv_ref[depth:])
    row_clip = lax.broadcasted_iota(jnp.int32, (rows, rows), 0) // tok
    col_clip = lax.broadcasted_iota(jnp.int32, (rows, rows), 1) // tok
    same_clip = row_clip == col_clip
    mixed = []
    for start in range(0, query.shape[1], HEAD_DIM):
        head = slice(start, start + HEAD_DIM)
        scores = lax.dot_general(
            query[:, head], keys[:, head], (((1,), (1,)), ((), ())), preferred_element_type=jnp.float32
        ) * (HEAD_DIM**-0.5)
        scores = jnp.where(same_clip, scores, -jnp.inf)
        weights = jnp.exp(scores - jnp.max(scores, -1, keepdims=True))
        weights = weights / jnp.sum(weights, -1, keepdims=True)
        mixed.append(project(weights.astype(jnp.bfloat16), values[:, head]))
    part = jnp.dot(jnp.concatenate(mixed, 1), wo_ref[...], preferred_element_type=jnp.float32)
    keep_ref[...] = part[:half]
    send_ref[...] = part[half:].astype(jnp.bfloat16)


def layer_part(mine, theirs, weights, tok):
    half, width = mine.shape[0] // 2, mine.shape[1]
    return pl.pallas_call(
        functools.partial(layer_kernel, tok),
        out_shape=(
            jax.ShapeDtypeStruct((half, width), jnp.float32),
            jax.ShapeDtypeStruct((half, width), jnp.bfloat16),
        ),
        in_specs=[pl.BlockSpec(memory_space=pltpu.VMEM)] * 5,
        out_specs=(pl.BlockSpec(memory_space=pltpu.VMEM),) * 2,
        compiler_params=pltpu.CompilerParams(vmem_limit_bytes=16 << 20),
    )(mine, theirs, *(pltpu.with_memory_space_constraint(w, pltpu.VMEM) for w in weights))


def entry_kernel(x_ref, gain_ref, normed_ref, x_out, gain_out, sems):
    copies = [
        pltpu.make_async_copy(x_ref, x_out, sems.at[0]),
        pltpu.make_async_copy(gain_ref, gain_out, sems.at[1]),
    ]
    for copy in copies:
        copy.start()
    for copy in copies:
        copy.wait()
    normed_ref[...] = normalized(x_out[...], gain_out[0])


def entry(state, gain):
    return pl.pallas_call(
        entry_kernel,
        out_shape=(
            pltpu.VMEM(state.shape, jnp.bfloat16),
            pltpu.VMEM(state.shape, state.dtype),
            pltpu.VMEM(gain.shape, gain.dtype),
        ),
        in_specs=[pl.BlockSpec(memory_space=pltpu.HBM)] * 2,
        out_specs=(pl.BlockSpec(memory_space=pltpu.VMEM),) * 3,
        scratch_shapes=[pltpu.SemaphoreType.DMA((2,))],
        compiler_params=pltpu.CompilerParams(vmem_limit_bytes=16 << 20),
    )(*in_hbm(state, gain))


def load_kernel(*refs):
    *refs, sems = refs
    count = len(refs) // 2
    copies = []
    for source, target in zip(refs[:count], refs[count:]):
        pieces = PIECES if source.shape[0] % (16 * PIECES) == 0 else 1
        rows = source.shape[0] // pieces
        for i in range(pieces):
            here = pl.ds(i * rows, rows)
            copies.append(pltpu.make_async_copy(source.at[here], target.at[here], sems.at[len(copies)]))
            copies[-1].start()
    for copy in copies:
        copy.wait()


def load(*arrays):
    return pl.pallas_call(
        load_kernel,
        out_shape=tuple(pltpu.VMEM(a.shape, a.dtype) for a in arrays),
        in_specs=[pl.BlockSpec(memory_space=pltpu.HBM)] * len(arrays),
        out_specs=(pl.BlockSpec(memory_space=pltpu.VMEM),) * len(arrays),
        scratch_shapes=[pltpu.SemaphoreType.DMA((PIECES * len(arrays),))],
        cost_estimate=pl.CostEstimate(
            flops=0, bytes_accessed=sum(a.size * a.dtype.itemsize for a in arrays), transcendentals=0
        ),
        compiler_params=pltpu.CompilerParams(vmem_limit_bytes=16 << 20),
    )(*in_hbm(*arrays))


def second_kernel(section_ref, offset_ref, handed_ref, fresh_ref, gain_ref, state_ref, normed_ref):
    tok = handed_ref.shape[0]
    picked = fresh_ref[pl.ds(pl.multiple_of(offset_ref[0] * tok, tok), tok)]
    state = jnp.where(section_ref[0] == 0, picked, handed_ref[...])
    state_ref[...] = state
    normed_ref[...] = normalized(state, gain_ref[0])


def second_entry(section, offsets, handed, fresh, gain):
    return pl.pallas_call(
        second_kernel,
        out_shape=(jax.ShapeDtypeStruct(handed.shape, handed.dtype),) * 2,
        in_specs=[pl.BlockSpec(memory_space=pltpu.SMEM)] * 2 + [pl.BlockSpec(memory_space=pltpu.VMEM)] * 3,
        out_specs=(pl.BlockSpec(memory_space=pltpu.VMEM),) * 2,
        compiler_params=pltpu.CompilerParams(vmem_limit_bytes=16 << 20),
    )(section, offsets, handed, fresh, gain)


def gathered(normed):
    lanes = lax.axis_size("lane")
    distances = [tower * lanes + 2 * k for tower in range(2) for k in range(lanes // 2)]
    blocks = {d: swapped(normed, d) if d else normed for d in distances}
    return jnp.concatenate([blocks[d] for d in distances], 0)


def reduced(state, keep, sent):
    tok = state.shape[0]
    total = keep + sent.astype(jnp.float32)
    result = state.astype(jnp.float32) + total[:tok]
    for k in range(1, lax.axis_size("lane") // 2):
        share = total[k * tok : (k + 1) * tok].astype(jnp.bfloat16)
        result = result + swapped(share, 2 * k).astype(jnp.float32)
    return result.astype(jnp.bfloat16)


def shards(in_flight, fresh_batches, offsets, norm_gain, w_query, w_keyval, w_out):
    normed, state, gain = entry(in_flight[0, 0], norm_gain[0])
    section = jnp.reshape(lax.axis_index("section"), (1,)).astype(jnp.int32)
    normed, section = lax.optimization_barrier((normed, section))
    wq, wkv = load(
        w_query[0, 0],
        w_keyval.reshape(-1, w_keyval.shape[-1]),
    )
    mine, wq, wkv = lax.optimization_barrier((gathered(normed), wq, wkv))
    wo, fresh = load(w_out[0, 0], fresh_batches.reshape(-1, fresh_batches.shape[-1]))
    weights = (wq, wkv, wo)
    keep, send = layer_part(mine, swapped(mine, 1), weights, state.shape[0])
    first = reduced(state, keep, swapped(send, 1))
    state, normed = second_entry(section, offsets, handed_on(first), fresh, gain)
    mine = gathered(normed)
    keep, send = layer_part(mine, swapped(mine, 1), weights, state.shape[0])
    second = reduced(state, keep, swapped(send, 1))
    return jnp.stack([first, second])[:, None, None]


def solution(mesh):
    placed = (
        P("section", "tower", "lane", None),
        P(None, "tower", "lane", None),
        P("lane"),
        P("section", "tower", None),
        P("section", "tower", None, "lane"),
        P("section", "tower", None, None, "lane"),
        P("section", "tower", "lane", None),
    )
    return jax.shard_map(
        shards,
        mesh=mesh,
        in_specs=placed,
        out_specs=P(None, "section", "tower", "lane", None),
        check_vma=False,
    )
```

```python
import functools

import jax
import jax.numpy as jnp
from jax import lax
from jax.experimental import pallas as pl
from jax.experimental.pallas import tpu as pltpu
from jax.sharding import PartitionSpec as P

HEAD_DIM = 128
EPSILON = 1e-06
BOTH = ("tower", "lane")
PIECES = 4


def swapped(value, mask):
    count = lax.axis_size(BOTH)
    return lax.ppermute(value, BOTH, [(i, i ^ mask) for i in range(count)])


def handed_on(value):
    count = lax.axis_size("section")
    return lax.ppermute(value, "section", [(s, s + 1) for s in range(count - 1)])


def in_hbm(*arrays):
    return [pltpu.with_memory_space_constraint(a, pltpu.HBM) for a in arrays]


def normalized(state, gain):
    wide = state.astype(jnp.float32)
    scale = lax.rsqrt(jnp.mean(wide * wide, -1, keepdims=True) + EPSILON)
    return (wide * scale * gain).astype(jnp.bfloat16)


def layer_kernel(tok, mine_ref, theirs_ref, wq_ref, wkv_ref, wo_ref, keep_ref, send_ref):
    half, depth = keep_ref.shape
    rows = 2 * half
    own = jnp.concatenate([mine_ref[half:], theirs_ref[half:]], 0)
    partner = jnp.concatenate([mine_ref[:half], theirs_ref[:half]], 0)

    def project(left, right):
        return jnp.dot(left, right, preferred_element_type=jnp.float32).astype(jnp.bfloat16)

    query = project(own, wq_ref[...])
    keys = project(partner, wkv_ref[:depth])
    values = project(partner, wkv_ref[depth:])
    row_clip = lax.broadcasted_iota(jnp.int32, (rows, rows), 0) // tok
    col_clip = lax.broadcasted_iota(jnp.int32, (rows, rows), 1) // tok
    same_clip = row_clip == col_clip
    mixed = []
    for start in range(0, query.shape[1], HEAD_DIM):
        head = slice(start, start + HEAD_DIM)
        scores = lax.dot_general(
            query[:, head], keys[:, head], (((1,), (1,)), ((), ())), preferred_element_type=jnp.float32
        ) * (HEAD_DIM**-0.5)
        scores = jnp.where(same_clip, scores, -jnp.inf)
        weights = jnp.exp(scores - jnp.max(scores, -1, keepdims=True))
        weights = weights / jnp.sum(weights, -1, keepdims=True)
        mixed.append(project(weights.astype(jnp.bfloat16), values[:, head]))
    part = jnp.dot(jnp.concatenate(mixed, 1), wo_ref[...], preferred_element_type=jnp.float32)
    keep_ref[...] = part[:half]
    send_ref[...] = part[half:].astype(jnp.bfloat16)


def layer_part(mine, theirs, weights, tok):
    half, width = mine.shape[0] // 2, mine.shape[1]
    return pl.pallas_call(
        functools.partial(layer_kernel, tok),
        out_shape=(
            jax.ShapeDtypeStruct((half, width), jnp.float32),
            jax.ShapeDtypeStruct((half, width), jnp.bfloat16),
        ),
        in_specs=[pl.BlockSpec(memory_space=pltpu.VMEM)] * 5,
        out_specs=(pl.BlockSpec(memory_space=pltpu.VMEM),) * 2,
        compiler_params=pltpu.CompilerParams(vmem_limit_bytes=16 << 20),
    )(mine, theirs, *(pltpu.with_memory_space_constraint(w, pltpu.VMEM) for w in weights))


def entry_kernel(x_ref, gain_ref, normed_ref, x_out, gain_out, sems):
    copies = [
        pltpu.make_async_copy(x_ref, x_out, sems.at[0]),
        pltpu.make_async_copy(gain_ref, gain_out, sems.at[1]),
    ]
    for copy in copies:
        copy.start()
    for copy in copies:
        copy.wait()
    normed_ref[...] = normalized(x_out[...], gain_out[0])


def entry(state, gain):
    return pl.pallas_call(
        entry_kernel,
        out_shape=(
            pltpu.VMEM(state.shape, jnp.bfloat16),
            pltpu.VMEM(state.shape, state.dtype),
            pltpu.VMEM(gain.shape, gain.dtype),
        ),
        in_specs=[pl.BlockSpec(memory_space=pltpu.HBM)] * 2,
        out_specs=(pl.BlockSpec(memory_space=pltpu.VMEM),) * 3,
        scratch_shapes=[pltpu.SemaphoreType.DMA((2,))],
        compiler_params=pltpu.CompilerParams(vmem_limit_bytes=16 << 20),
    )(*in_hbm(state, gain))


def load_kernel(*refs):
    *refs, sems = refs
    count = len(refs) // 2
    copies = []
    for source, target in zip(refs[:count], refs[count:]):
        pieces = PIECES if source.shape[0] % (16 * PIECES) == 0 else 1
        rows = source.shape[0] // pieces
        for i in range(pieces):
            here = pl.ds(i * rows, rows)
            copies.append(pltpu.make_async_copy(source.at[here], target.at[here], sems.at[len(copies)]))
            copies[-1].start()
    for copy in copies:
        copy.wait()


def load(*arrays):
    return pl.pallas_call(
        load_kernel,
        out_shape=tuple(pltpu.VMEM(a.shape, a.dtype) for a in arrays),
        in_specs=[pl.BlockSpec(memory_space=pltpu.HBM)] * len(arrays),
        out_specs=(pl.BlockSpec(memory_space=pltpu.VMEM),) * len(arrays),
        scratch_shapes=[pltpu.SemaphoreType.DMA((PIECES * len(arrays),))],
        cost_estimate=pl.CostEstimate(
            flops=0, bytes_accessed=sum(a.size * a.dtype.itemsize for a in arrays), transcendentals=0
        ),
        compiler_params=pltpu.CompilerParams(vmem_limit_bytes=16 << 20),
    )(*in_hbm(*arrays))


def second_kernel(section_ref, offset_ref, handed_ref, fresh_ref, gain_ref, state_ref, normed_ref):
    tok = handed_ref.shape[0]
    picked = fresh_ref[pl.ds(pl.multiple_of(offset_ref[0] * tok, tok), tok)]
    state = jnp.where(section_ref[0] == 0, picked, handed_ref[...])
    state_ref[...] = state
    normed_ref[...] = normalized(state, gain_ref[0])


def second_entry(section, offsets, handed, fresh, gain):
    return pl.pallas_call(
        second_kernel,
        out_shape=(jax.ShapeDtypeStruct(handed.shape, handed.dtype),) * 2,
        in_specs=[pl.BlockSpec(memory_space=pltpu.SMEM)] * 2 + [pl.BlockSpec(memory_space=pltpu.VMEM)] * 3,
        out_specs=(pl.BlockSpec(memory_space=pltpu.VMEM),) * 2,
        compiler_params=pltpu.CompilerParams(vmem_limit_bytes=16 << 20),
    )(section, offsets, handed, fresh, gain)


def gathered(normed):
    lanes = lax.axis_size("lane")
    distances = [tower * lanes + 2 * k for tower in range(2) for k in range(lanes // 2)]
    return jnp.concatenate([swapped(normed, d) if d else normed for d in reversed(distances)], 0)


def reduced(state, keep, sent):
    tok = state.shape[0]
    total = keep + sent.astype(jnp.float32)
    blocks = list(reversed(jnp.split(total, keep.shape[0] // tok)))
    result = state.astype(jnp.float32) + blocks[0]
    for k in range(1, len(blocks)):
        result = result + swapped(blocks[k].astype(jnp.bfloat16), 2 * k).astype(jnp.float32)
    return result.astype(jnp.bfloat16)


def shards(in_flight, fresh_batches, offsets, norm_gain, w_query, w_keyval, w_out):
    normed, state, gain = entry(in_flight[0, 0], norm_gain[0])
    section = jnp.reshape(lax.axis_index("section"), (1,)).astype(jnp.int32)
    normed, section = lax.optimization_barrier((normed, section))
    wq, wkv = load(
        w_query[0, 0],
        w_keyval.reshape(-1, w_keyval.shape[-1]),
    )
    mine, wq, wkv = lax.optimization_barrier((gathered(normed), wq, wkv))
    wo, fresh = load(w_out[0, 0], fresh_batches.reshape(-1, fresh_batches.shape[-1]))
    weights = (wq, wkv, wo)
    keep, send = layer_part(mine, swapped(mine, 1), weights, state.shape[0])
    first = reduced(state, keep, swapped(send, 1))
    state, normed = second_entry(section, offsets, handed_on(first), fresh, gain)
    mine = gathered(normed)
    keep, send = layer_part(mine, swapped(mine, 1), weights, state.shape[0])
    second = reduced(state, keep, swapped(send, 1))
    return jnp.stack([first, second])[:, None, None]


def solution(mesh):
    placed = (
        P("section", "tower", "lane", None),
        P(None, "tower", "lane", None),
        P("lane"),
        P("section", "tower", None),
        P("section", "tower", None, "lane"),
        P("section", "tower", None, None, "lane"),
        P("section", "tower", "lane", None),
    )
    return jax.shard_map(
        shards,
        mesh=mesh,
        in_specs=placed,
        out_specs=P(None, "section", "tower", "lane", None),
        check_vma=False,
    )
```

```python
import functools

import jax
import jax.numpy as jnp
from jax import lax
from jax.experimental import pallas as pl
from jax.experimental.pallas import tpu as pltpu
from jax.sharding import PartitionSpec as P

HEAD_DIM = 128
EPSILON = 1e-06
BOTH = ("tower", "lane")
PIECES = 4


def swapped(value, mask):
    count = lax.axis_size(BOTH)
    return lax.ppermute(value, BOTH, [(i, i ^ mask) for i in range(count)])


def climbed(value, hop):
    sections, lanes = lax.axis_size("section"), lax.axis_size("lane")
    results = []
    for climbs in range(2):
        pairs = []
        for s in range(sections):
            for lane in range(lanes):
                to, target = (s + 1, lane ^ hop) if lane % 2 == climbs else (s - 1, lane)
                if not 0 <= to < sections:
                    to, target = s, lane ^ 1
                pairs.append((s * lanes + lane, to * lanes + target))
        results.append(lax.ppermute(value, ("section", "lane"), pairs))
    return results


def in_hbm(*arrays):
    return [pltpu.with_memory_space_constraint(a, pltpu.HBM) for a in arrays]


def normalized(state, gain):
    wide = state.astype(jnp.float32)
    scale = lax.rsqrt(jnp.mean(wide * wide, -1, keepdims=True) + EPSILON)
    return (wide * scale * gain).astype(jnp.bfloat16)


def project(left, right):
    return jnp.dot(left, right, preferred_element_type=jnp.float32).astype(jnp.bfloat16)


def keyval_kernel(mine_ref, theirs_ref, wkv_ref, keys_ref, values_ref):
    depth = mine_ref.shape[1]
    partner = jnp.concatenate([mine_ref[...], theirs_ref[...]], 0)
    keys_ref[...] = project(partner, wkv_ref[:depth])
    values_ref[...] = project(partner, wkv_ref[depth:])


def attend_kernel(tok, mine_ref, theirs_ref, keys_ref, values_ref, wq_ref, wo_ref, keep_ref, send_ref):
    half = keep_ref.shape[0]
    rows = 2 * half
    query = project(jnp.concatenate([mine_ref[...], theirs_ref[...]], 0), wq_ref[...])
    row_clip = lax.broadcasted_iota(jnp.int32, (rows, rows), 0) // tok
    col_clip = lax.broadcasted_iota(jnp.int32, (rows, rows), 1) // tok
    same_clip = row_clip == col_clip
    mixed = []
    for start in range(0, query.shape[1], HEAD_DIM):
        head = slice(start, start + HEAD_DIM)
        scores = lax.dot_general(
            query[:, head], keys_ref[:, head], (((1,), (1,)), ((), ())), preferred_element_type=jnp.float32
        ) * (HEAD_DIM**-0.5)
        scores = jnp.where(same_clip, scores, -jnp.inf)
        weights = jnp.exp(scores - jnp.max(scores, -1, keepdims=True))
        weights = weights / jnp.sum(weights, -1, keepdims=True)
        mixed.append(project(weights.astype(jnp.bfloat16), values_ref[:, head]))
    part = jnp.dot(jnp.concatenate(mixed, 1), wo_ref[...], preferred_element_type=jnp.float32)
    keep_ref[...] = part[:half]
    send_ref[...] = part[half:].astype(jnp.bfloat16)


def in_vmem(*arrays):
    return [pltpu.with_memory_space_constraint(a, pltpu.VMEM) for a in arrays]


def on_chip(kernel, outs, *arrays, flops=0):
    size = sum(a.size * a.dtype.itemsize for a in arrays)
    return pl.pallas_call(
        kernel,
        out_shape=tuple(jax.ShapeDtypeStruct(shape, dtype) for shape, dtype in outs),
        in_specs=[pl.BlockSpec(memory_space=pltpu.VMEM)] * len(arrays),
        out_specs=(pl.BlockSpec(memory_space=pltpu.VMEM),) * len(outs),
        cost_estimate=pl.CostEstimate(flops=flops, bytes_accessed=size, transcendentals=0),
        compiler_params=pltpu.CompilerParams(vmem_limit_bytes=16 << 20),
    )(*arrays)


def layer_part(own, partner, weights, tok):
    wq, wkv, wo = weights[0], *in_vmem(weights[1]), weights[2]
    (half, width), head_cols = own.shape, wq.shape[1]
    partner_theirs = swapped(partner, 1)
    own_theirs = swapped(own, 1)
    pushed = 2 * 256 * width * head_cols
    keys, values = on_chip(
        keyval_kernel,
        [((2 * half, head_cols), jnp.bfloat16)] * 2,
        partner, partner_theirs, wkv,
        flops=2 * pushed,
    )
    return on_chip(
        functools.partial(attend_kernel, tok),
        [((half, width), jnp.float32), ((half, width), jnp.bfloat16)],
        own, own_theirs, keys, values, wq, wo,
        flops=3 * pushed,
    )


def sum_kernel(state_ref, keep_ref, sent_ref, own_ref, *out_refs):
    tok = state_ref.shape[0]
    total = keep_ref[...] + sent_ref[...].astype(jnp.float32)
    own_ref[...] = state_ref[...].astype(jnp.float32) + total[-tok:]
    for k, out_ref in enumerate(out_refs, 1):
        start = total.shape[0] - (k + 1) * tok
        out_ref[...] = total[start : start + tok].astype(jnp.bfloat16)


def entry_kernel(x_ref, gain_ref, normed_ref, x_out, gain_out, sems):
    copies = [
        pltpu.make_async_copy(x_ref, x_out, sems.at[0]),
        pltpu.make_async_copy(gain_ref, gain_out, sems.at[1]),
    ]
    for copy in copies:
        copy.start()
    for copy in copies:
        copy.wait()
    normed_ref[...] = normalized(x_out[...], gain_out[0])


def entry(state, gain):
    return pl.pallas_call(
        entry_kernel,
        out_shape=(
            pltpu.VMEM(state.shape, jnp.bfloat16),
            pltpu.VMEM(state.shape, state.dtype),
            pltpu.VMEM(gain.shape, gain.dtype),
        ),
        in_specs=[pl.BlockSpec(memory_space=pltpu.HBM)] * 2,
        out_specs=(pl.BlockSpec(memory_space=pltpu.VMEM),) * 3,
        scratch_shapes=[pltpu.SemaphoreType.DMA((2,))],
        compiler_params=pltpu.CompilerParams(vmem_limit_bytes=16 << 20),
    )(*in_hbm(state, gain))


def load_kernel(*refs):
    *refs, sems = refs
    count = len(refs) // 2
    copies = []
    for source, target in zip(refs[:count], refs[count:]):
        pieces = PIECES if source.shape[0] % (16 * PIECES) == 0 else 1
        rows = source.shape[0] // pieces
        for i in range(pieces):
            here = pl.ds(i * rows, rows)
            copies.append(pltpu.make_async_copy(source.at[here], target.at[here], sems.at[len(copies)]))
            copies[-1].start()
    for copy in copies:
        copy.wait()


def load(*arrays):
    return pl.pallas_call(
        load_kernel,
        out_shape=tuple(pltpu.VMEM(a.shape, a.dtype) for a in arrays),
        in_specs=[pl.BlockSpec(memory_space=pltpu.HBM)] * len(arrays),
        out_specs=(pl.BlockSpec(memory_space=pltpu.VMEM),) * len(arrays),
        scratch_shapes=[pltpu.SemaphoreType.DMA((PIECES * len(arrays),))],
        cost_estimate=pl.CostEstimate(
            flops=0, bytes_accessed=sum(a.size * a.dtype.itemsize for a in arrays), transcendentals=0
        ),
        compiler_params=pltpu.CompilerParams(vmem_limit_bytes=16 << 20),
    )(*in_hbm(*arrays))


def second_kernel(section_ref, lane_ref, offset_ref, fresh_ref, gain_ref, *refs):
    *handed_refs, state_ref, normed_ref = refs
    tok = state_ref.shape[0]
    even = lane_ref[0] % 2 == 0
    handed = 0.0
    for even_ref, odd_ref in zip(handed_refs[::2], handed_refs[1::2]):
        handed = handed + jnp.where(even, even_ref[...], odd_ref[...]).astype(jnp.float32)
    picked = fresh_ref[pl.ds(pl.multiple_of(offset_ref[0] * tok, tok), tok)]
    state = jnp.where(section_ref[0] == 0, picked, handed.astype(jnp.bfloat16))
    state_ref[...] = state
    normed_ref[...] = normalized(state, gain_ref[0])


def second_entry(section, lane, offsets, fresh, gain, handed):
    shape = handed[0].shape
    return pl.pallas_call(
        second_kernel,
        out_shape=(pltpu.VMEM(shape, jnp.bfloat16),) * 2,
        in_specs=[pl.BlockSpec(memory_space=pltpu.SMEM)] * 3
        + [pl.BlockSpec(memory_space=pltpu.VMEM)] * (2 + len(handed)),
        out_specs=(pl.BlockSpec(memory_space=pltpu.VMEM),) * 2,
        compiler_params=pltpu.CompilerParams(vmem_limit_bytes=16 << 20),
    )(section, lane, offsets, fresh, gain, *handed)


def gathered(normed):
    lanes = lax.axis_size("lane")
    towers = [[tower * lanes + 2 * k for k in reversed(range(lanes // 2))] for tower in range(2)]
    partner = [swapped(normed, d) for d in towers[1]]
    own = [swapped(normed, d) if d else normed for d in towers[0]]
    return jnp.concatenate(own, 0), jnp.concatenate(partner, 0)


def summed(state, keep, send):
    shape = state.shape
    outs = [(shape, jnp.float32)] + [(shape, jnp.bfloat16)] * (keep.shape[0] // shape[0] - 1)
    own, *others = on_chip(sum_kernel, outs, *in_vmem(state), keep, swapped(send, 1))
    return own, others


def completed(own, others):
    for k, other in enumerate(others, 1):
        own = own + swapped(other, 2 * k).astype(jnp.float32)
    return own.astype(jnp.bfloat16)


def index_of(axis):
    return jnp.reshape(lax.axis_index(axis), (1,)).astype(jnp.int32)


def shards(in_flight, fresh_batches, offsets, norm_gain, w_query, w_keyval, w_out):
    normed, state, gain = entry(in_flight[0, 0], norm_gain[0])
    tok = state.shape[0]
    normed, section, lane = lax.optimization_barrier((normed, index_of("section"), index_of("lane")))
    (wkv,) = load(w_keyval.reshape(-1, w_keyval.shape[-1]))
    own, partner, wkv = lax.optimization_barrier((*gathered(normed), wkv))
    wq, wo, fresh = w_query[0, 0], w_out[0, 0], fresh_batches.reshape(-1, fresh_batches.shape[-1])
    weights = (wq, wkv, wo)
    first_sum, others = summed(state, *layer_part(own, partner, weights, tok))
    sums = [first_sum.astype(jnp.bfloat16), *others]
    handed = [part for k in reversed(range(len(sums))) for part in climbed(sums[k], 2 * k)]
    state, normed = second_entry(section, lane, offsets, fresh, gain, handed)
    own, partner = gathered(normed)
    own, others = lax.optimization_barrier((own, others))
    keep, send, first_sum = lax.optimization_barrier((*layer_part(own, partner, weights, tok), first_sum))
    first = completed(first_sum, others)
    keep, send, first = lax.optimization_barrier((keep, send, first))
    second = completed(*summed(state, keep, send))
    return jnp.stack([first, second])[:, None, None]


def solution(mesh):
    placed = (
        P("section", "tower", "lane", None),
        P(None, "tower", "lane", None),
        P("lane"),
        P("section", "tower", None),
        P("section", "tower", None, "lane"),
        P("section", "tower", None, None, "lane"),
        P("section", "tower", "lane", None),
    )
    return jax.shard_map(
        shards,
        mesh=mesh,
        in_specs=placed,
        out_specs=P(None, "section", "tower", "lane", None),
        check_vma=False,
    )
```

```python
import functools

import jax
import jax.numpy as jnp
from jax import lax
from jax.experimental import pallas as pl
from jax.experimental.pallas import tpu as pltpu
from jax.sharding import PartitionSpec as P

HEAD_DIM = 128
EPSILON = 1e-06
BOTH = ("tower", "lane")
PIECES = 4


def swapped(value, mask):
    count = lax.axis_size(BOTH)
    return lax.ppermute(value, BOTH, [(i, i ^ mask) for i in range(count)])


def climbed(value, hop, climbs):
    sections, lanes = lax.axis_size("section"), lax.axis_size("lane")
    pairs = []
    for s in range(sections):
        for lane in range(lanes):
            to, target = (s + 1, lane ^ hop) if lane % 2 == climbs else (s - 1, lane)
            if not 0 <= to < sections:
                to, target = s, lane ^ 1
            pairs.append((s * lanes + lane, to * lanes + target))
    return lax.ppermute(value, ("section", "lane"), pairs)


def handed_on(own, others):
    blocks = [climbed(own, 0, 0), climbed(own, 0, 1)]
    for k, other in enumerate(others, 1):
        blocks += [swapped(other, 2 * k), climbed(other, 2 * k, 1), climbed(other, 2 * k, 0)]
    return jnp.concatenate(blocks, 0)


def in_hbm(*arrays):
    return [pltpu.with_memory_space_constraint(a, pltpu.HBM) for a in arrays]


def normalized(state, gain):
    wide = state.astype(jnp.float32)
    scale = lax.rsqrt(jnp.mean(wide * wide, -1, keepdims=True) + EPSILON)
    return (wide * scale * gain).astype(jnp.bfloat16)


def project(left, right):
    return jnp.dot(left, right, preferred_element_type=jnp.float32).astype(jnp.bfloat16)


def keyval_kernel(mine_ref, theirs_ref, wkv_ref, keys_ref, values_ref):
    depth = mine_ref.shape[1]
    partner = jnp.concatenate([mine_ref[...], theirs_ref[...]], 0)
    keys_ref[...] = project(partner, wkv_ref[:depth])
    values_ref[...] = project(partner, wkv_ref[depth:])


def attend_kernel(tok, mine_ref, theirs_ref, keys_ref, values_ref, wq_ref, wo_ref, keep_ref, send_ref):
    half, width = keep_ref.shape
    rows = 2 * half
    query = project(jnp.concatenate([mine_ref[...], theirs_ref[...]], 0), wq_ref[...])
    row_clip = lax.broadcasted_iota(jnp.int32, (rows, rows), 0) // tok
    col_clip = lax.broadcasted_iota(jnp.int32, (rows, rows), 1) // tok
    same_clip = row_clip == col_clip
    heads = [slice(start, start + HEAD_DIM) for start in range(0, query.shape[1], HEAD_DIM)]
    scores = [
        lax.dot_general(
            query[:, head], keys_ref[:, head], (((1,), (1,)), ((), ())), preferred_element_type=jnp.float32
        )
        for head in heads
    ]
    scores = [jnp.where(same_clip, score * (HEAD_DIM**-0.5), -jnp.inf) for score in scores]
    tops = [jnp.max(score, -1, keepdims=True) for score in scores]
    weights = [jnp.exp(score - top).astype(jnp.bfloat16) for score, top in zip(scores, tops)]
    ones = jnp.ones((rows, HEAD_DIM), jnp.bfloat16)
    sums = [jnp.dot(weight, ones, preferred_element_type=jnp.float32) for weight in weights]
    mixed = [
        jnp.dot(weight, values_ref[:, head], preferred_element_type=jnp.float32)
        for weight, head in zip(weights, heads)
    ]
    mixed = jnp.concatenate([(mix / total).astype(jnp.bfloat16) for mix, total in zip(mixed, sums)], 1)
    for start in range(0, width, width // 4):
        columns = slice(start, start + width // 4)
        part = jnp.dot(mixed, wo_ref[:, columns], preferred_element_type=jnp.float32)
        keep_ref[:, columns] = part[:half]
        send_ref[:, columns] = part[half:].astype(jnp.bfloat16)


def in_vmem(*arrays):
    return [pltpu.with_memory_space_constraint(a, pltpu.VMEM) for a in arrays]


def on_chip(kernel, outs, *arrays, flops=0):
    size = sum(a.size * a.dtype.itemsize for a in arrays)
    return pl.pallas_call(
        kernel,
        out_shape=tuple(jax.ShapeDtypeStruct(shape, dtype) for shape, dtype in outs),
        in_specs=[pl.BlockSpec(memory_space=pltpu.VMEM)] * len(arrays),
        out_specs=(pl.BlockSpec(memory_space=pltpu.VMEM),) * len(outs),
        cost_estimate=pl.CostEstimate(flops=flops, bytes_accessed=size, transcendentals=0),
        compiler_params=pltpu.CompilerParams(vmem_limit_bytes=16 << 20),
    )(*arrays)


def layer_part(own, partner, weights, tok):
    wq, wkv, wo = weights[0], *in_vmem(weights[1]), weights[2]
    (half, width), head_cols = own.shape, wq.shape[1]
    partner_theirs = swapped(partner, 1)
    own_theirs = swapped(own, 1)
    pushed = 2 * 256 * width * head_cols
    keys, values = on_chip(
        keyval_kernel,
        [((2 * half, head_cols), jnp.bfloat16)] * 2,
        partner, partner_theirs, wkv,
        flops=2 * pushed,
    )
    return on_chip(
        functools.partial(attend_kernel, tok),
        [((half, width), jnp.float32), ((half, width), jnp.bfloat16)],
        own, own_theirs, keys, values, wq, wo,
        flops=3 * pushed,
    )


def sum_kernel(state_ref, keep_ref, sent_ref, own_ref, *out_refs):
    tok = state_ref.shape[0]
    total = keep_ref[...] + sent_ref[...].astype(jnp.float32)
    own_ref[...] = state_ref[...].astype(jnp.float32) + total[-tok:]
    for k, out_ref in enumerate(out_refs, 1):
        start = total.shape[0] - (k + 1) * tok
        out_ref[...] = total[start : start + tok].astype(jnp.bfloat16)


def entry_kernel(x_ref, gain_ref, normed_ref, x_out, gain_out, sems):
    copies = [
        pltpu.make_async_copy(x_ref, x_out, sems.at[0]),
        pltpu.make_async_copy(gain_ref, gain_out, sems.at[1]),
    ]
    for copy in copies:
        copy.start()
    for copy in copies:
        copy.wait()
    normed_ref[...] = normalized(x_out[...], gain_out[0])


def entry(state, gain):
    return pl.pallas_call(
        entry_kernel,
        out_shape=(
            pltpu.VMEM(state.shape, jnp.bfloat16),
            pltpu.VMEM(state.shape, state.dtype),
            pltpu.VMEM(gain.shape, gain.dtype),
        ),
        in_specs=[pl.BlockSpec(memory_space=pltpu.HBM)] * 2,
        out_specs=(pl.BlockSpec(memory_space=pltpu.VMEM),) * 3,
        scratch_shapes=[pltpu.SemaphoreType.DMA((2,))],
        compiler_params=pltpu.CompilerParams(vmem_limit_bytes=16 << 20),
    )(*in_hbm(state, gain))


def load_kernel(*refs):
    *refs, sems = refs
    count = len(refs) // 2
    copies = []
    for source, target in zip(refs[:count], refs[count:]):
        pieces = PIECES if source.shape[0] % (16 * PIECES) == 0 else 1
        rows = source.shape[0] // pieces
        for i in range(pieces):
            here = pl.ds(i * rows, rows)
            copies.append(pltpu.make_async_copy(source.at[here], target.at[here], sems.at[len(copies)]))
            copies[-1].start()
    for copy in copies:
        copy.wait()


def load(*arrays):
    return pl.pallas_call(
        load_kernel,
        out_shape=tuple(pltpu.VMEM(a.shape, a.dtype) for a in arrays),
        in_specs=[pl.BlockSpec(memory_space=pltpu.HBM)] * len(arrays),
        out_specs=(pl.BlockSpec(memory_space=pltpu.VMEM),) * len(arrays),
        scratch_shapes=[pltpu.SemaphoreType.DMA((PIECES * len(arrays),))],
        cost_estimate=pl.CostEstimate(
            flops=0, bytes_accessed=sum(a.size * a.dtype.itemsize for a in arrays), transcendentals=0
        ),
        compiler_params=pltpu.CompilerParams(vmem_limit_bytes=16 << 20),
    )(*in_hbm(*arrays))


def second_kernel(
    section_ref, lane_ref, offset_ref, fresh_ref, gain_ref, own_ref, handed_ref, first_ref, state_ref, normed_ref
):
    tok = state_ref.shape[0]

    def block(index):
        return handed_ref[pl.ds(pl.multiple_of(index * tok, tok), tok)].astype(jnp.float32)

    odd = lane_ref[0] % 2
    first, handed = own_ref[...], block(odd)
    for index in range(2, handed_ref.shape[0] // tok, 3):
        first = first + block(index)
        handed = handed + block(index + 2 - odd)
    first_ref[...] = first.astype(jnp.bfloat16)
    picked = fresh_ref[pl.ds(pl.multiple_of(offset_ref[0] * tok, tok), tok)]
    state = jnp.where(section_ref[0] == 0, picked, handed.astype(jnp.bfloat16))
    state_ref[...] = state
    normed_ref[...] = normalized(state, gain_ref[0])


def second_entry(section, lane, offsets, fresh, gain, own, handed):
    return pl.pallas_call(
        second_kernel,
        out_shape=(pltpu.VMEM(own.shape, jnp.bfloat16),) * 3,
        in_specs=[pl.BlockSpec(memory_space=pltpu.SMEM)] * 3 + [pl.BlockSpec(memory_space=pltpu.VMEM)] * 4,
        out_specs=(pl.BlockSpec(memory_space=pltpu.VMEM),) * 3,
        compiler_params=pltpu.CompilerParams(vmem_limit_bytes=16 << 20),
    )(section, lane, offsets, fresh, gain, own, handed)


def gathered(normed):
    lanes = lax.axis_size("lane")
    towers = [[tower * lanes + 2 * k for k in reversed(range(lanes // 2))] for tower in range(2)]
    partner = [swapped(normed, d) for d in towers[1]]
    own = [swapped(normed, d) if d else normed for d in towers[0]]
    return jnp.concatenate(own, 0), jnp.concatenate(partner, 0)


def summed(state, keep, send):
    shape = state.shape
    outs = [(shape, jnp.float32)] + [(shape, jnp.bfloat16)] * (keep.shape[0] // shape[0] - 1)
    own, *others = on_chip(sum_kernel, outs, *in_vmem(state), keep, swapped(send, 1))
    return own, others


def completed(own, others):
    for k, other in enumerate(others, 1):
        own = own + swapped(other, 2 * k).astype(jnp.float32)
    return own.astype(jnp.bfloat16)


def index_of(axis):
    return jnp.reshape(lax.axis_index(axis), (1,)).astype(jnp.int32)


def shards(in_flight, fresh_batches, offsets, norm_gain, w_query, w_keyval, w_out):
    normed, state, gain = entry(in_flight[0, 0], norm_gain[0])
    tok = state.shape[0]
    normed, section, lane = lax.optimization_barrier((normed, index_of("section"), index_of("lane")))
    (wkv,) = load(w_keyval.reshape(-1, w_keyval.shape[-1]))
    own, partner = gathered(normed)
    partner, wkv = lax.optimization_barrier((partner, wkv))
    wq, wo, fresh = w_query[0, 0], w_out[0, 0], fresh_batches.reshape(-1, fresh_batches.shape[-1])
    weights = (wq, wkv, wo)
    first_sum, others = summed(state, *layer_part(own, partner, weights, tok))
    handed = handed_on(first_sum.astype(jnp.bfloat16), others)
    first, state, normed = second_entry(section, lane, offsets, fresh, gain, first_sum, handed)
    own, partner = gathered(normed)
    second = completed(*summed(state, *layer_part(own, partner, weights, tok)))
    return jnp.stack([first, second])[:, None, None]


def solution(mesh):
    placed = (
        P("section", "tower", "lane", None),
        P(None, "tower", "lane", None),
        P("lane"),
        P("section", "tower", None),
        P("section", "tower", None, "lane"),
        P("section", "tower", None, None, "lane"),
        P("section", "tower", "lane", None),
    )
    return jax.shard_map(
        shards,
        mesh=mesh,
        in_specs=placed,
        out_specs=P(None, "section", "tower", "lane", None),
        check_vma=False,
    )
```

```python
import functools

import jax
import jax.numpy as jnp
from jax import lax
from jax.experimental import pallas as pl
from jax.experimental.pallas import tpu as pltpu
from jax.sharding import PartitionSpec as P

HEAD_DIM = 128
EPSILON = 1e-06
BOTH = ("tower", "lane")
PIECES = 4


def swapped(value, mask):
    count = lax.axis_size(BOTH)
    return lax.ppermute(value, BOTH, [(i, i ^ mask) for i in range(count)])


def climbed(value, hop, climbs):
    sections, lanes = lax.axis_size("section"), lax.axis_size("lane")
    pairs = []
    for s in range(sections):
        for lane in range(lanes):
            to, target = (s + 1, lane ^ hop) if lane % 2 == climbs else (s - 1, lane)
            if not 0 <= to < sections:
                to, target = s, lane ^ 1
            pairs.append((s * lanes + lane, to * lanes + target))
    return lax.ppermute(value, ("section", "lane"), pairs)


def handed_on(own, others):
    blocks = [climbed(own, 0, 0), climbed(own, 0, 1)]
    for k, other in enumerate(others, 1):
        blocks += [swapped(other, 2 * k), climbed(other, 2 * k, 1), climbed(other, 2 * k, 0)]
    return jnp.concatenate(blocks, 0)


def in_hbm(*arrays):
    return [pltpu.with_memory_space_constraint(a, pltpu.HBM) for a in arrays]


def normalized(state, gain):
    wide = state.astype(jnp.float32)
    scale = lax.rsqrt(jnp.mean(wide * wide, -1, keepdims=True) + EPSILON)
    return (wide * scale * gain).astype(jnp.bfloat16)


def project(left, right):
    return jnp.dot(left, right, preferred_element_type=jnp.float32).astype(jnp.bfloat16)


def query_kernel(mine_ref, theirs_ref, wq_ref, query_ref):
    query_ref[...] = project(jnp.concatenate([mine_ref[...], theirs_ref[...]], 0), wq_ref[...])


def attend_kernel(tok, mine_ref, theirs_ref, query_ref, wkv_ref, wo_ref, keep_ref, send_ref):
    half, width = keep_ref.shape
    rows = 2 * half
    partner = jnp.concatenate([mine_ref[...], theirs_ref[...]], 0)
    keys = project(partner, wkv_ref[:width])
    values = project(partner, wkv_ref[width:])
    row_clip = lax.broadcasted_iota(jnp.int32, (rows, rows), 0) // tok
    col_clip = lax.broadcasted_iota(jnp.int32, (rows, rows), 1) // tok
    same_clip = row_clip == col_clip
    heads = [slice(start, start + HEAD_DIM) for start in range(0, keys.shape[1], HEAD_DIM)]
    scores = [
        lax.dot_general(
            query_ref[:, head], keys[:, head], (((1,), (1,)), ((), ())), preferred_element_type=jnp.float32
        )
        for head in heads
    ]
    scores = [jnp.where(same_clip, score * (HEAD_DIM**-0.5), -jnp.inf) for score in scores]
    tops = [jnp.max(score, -1, keepdims=True) for score in scores]
    weights = [jnp.exp(score - top).astype(jnp.bfloat16) for score, top in zip(scores, tops)]
    ones = jnp.ones((rows, HEAD_DIM), jnp.bfloat16)
    sums = [jnp.dot(weight, ones, preferred_element_type=jnp.float32) for weight in weights]
    mixed = [
        jnp.dot(weight, values[:, head], preferred_element_type=jnp.float32)
        for weight, head in zip(weights, heads)
    ]
    mixed = jnp.concatenate([(mix / total).astype(jnp.bfloat16) for mix, total in zip(mixed, sums)], 1)
    for start in range(0, width, width // 4):
        columns = slice(start, start + width // 4)
        part = jnp.dot(mixed, wo_ref[:, columns], preferred_element_type=jnp.float32)
        keep_ref[:, columns] = part[:half]
        send_ref[:, columns] = part[half:].astype(jnp.bfloat16)


def in_vmem(*arrays):
    return [pltpu.with_memory_space_constraint(a, pltpu.VMEM) for a in arrays]


def on_chip(kernel, outs, *arrays, flops=0):
    size = sum(a.size * a.dtype.itemsize for a in arrays)
    return pl.pallas_call(
        kernel,
        out_shape=tuple(jax.ShapeDtypeStruct(shape, dtype) for shape, dtype in outs),
        in_specs=[pl.BlockSpec(memory_space=pltpu.VMEM)] * len(arrays),
        out_specs=(pl.BlockSpec(memory_space=pltpu.VMEM),) * len(outs),
        cost_estimate=pl.CostEstimate(flops=flops, bytes_accessed=size, transcendentals=0),
        compiler_params=pltpu.CompilerParams(vmem_limit_bytes=16 << 20),
    )(*arrays)


def layer_part(own, partner, weights, tok):
    wq, wkv, wo = weights[0], *in_vmem(weights[1]), weights[2]
    (half, width), head_cols = own.shape, wq.shape[1]
    pushed = 2 * 256 * width * head_cols
    (query,) = on_chip(
        query_kernel, [((2 * half, head_cols), jnp.bfloat16)], own, swapped(own, 1), wq, flops=pushed
    )
    return on_chip(
        functools.partial(attend_kernel, tok),
        [((half, width), jnp.float32), ((half, width), jnp.bfloat16)],
        partner, swapped(partner, 1), query, wkv, wo,
        flops=4 * pushed,
    )


def sum_kernel(state_ref, keep_ref, sent_ref, own_ref, *out_refs):
    tok = state_ref.shape[0]
    total = keep_ref[...] + sent_ref[...].astype(jnp.float32)
    own_ref[...] = state_ref[...].astype(jnp.float32) + total[:tok]
    for k, out_ref in enumerate(out_refs, 1):
        out_ref[...] = total[k * tok : (k + 1) * tok].astype(jnp.bfloat16)


def entry_kernel(x_ref, gain_ref, normed_ref, x_out, gain_out, sems):
    copies = [
        pltpu.make_async_copy(x_ref, x_out, sems.at[0]),
        pltpu.make_async_copy(gain_ref, gain_out, sems.at[1]),
    ]
    for copy in copies:
        copy.start()
    for copy in copies:
        copy.wait()
    normed_ref[...] = normalized(x_out[...], gain_out[0])


def entry(state, gain):
    return pl.pallas_call(
        entry_kernel,
        out_shape=(
            pltpu.VMEM(state.shape, jnp.bfloat16),
            pltpu.VMEM(state.shape, state.dtype),
            pltpu.VMEM(gain.shape, gain.dtype),
        ),
        in_specs=[pl.BlockSpec(memory_space=pltpu.HBM)] * 2,
        out_specs=(pl.BlockSpec(memory_space=pltpu.VMEM),) * 3,
        scratch_shapes=[pltpu.SemaphoreType.DMA((2,))],
        compiler_params=pltpu.CompilerParams(vmem_limit_bytes=16 << 20),
    )(*in_hbm(state, gain))


def load_kernel(*refs):
    *refs, sems = refs
    count = len(refs) // 2
    copies = []
    for source, target in zip(refs[:count], refs[count:]):
        pieces = PIECES if source.shape[0] % (16 * PIECES) == 0 else 1
        rows = source.shape[0] // pieces
        for i in range(pieces):
            here = pl.ds(i * rows, rows)
            copies.append(pltpu.make_async_copy(source.at[here], target.at[here], sems.at[len(copies)]))
            copies[-1].start()
    for copy in copies:
        copy.wait()


def load(*arrays):
    return pl.pallas_call(
        load_kernel,
        out_shape=tuple(pltpu.VMEM(a.shape, a.dtype) for a in arrays),
        in_specs=[pl.BlockSpec(memory_space=pltpu.HBM)] * len(arrays),
        out_specs=(pl.BlockSpec(memory_space=pltpu.VMEM),) * len(arrays),
        scratch_shapes=[pltpu.SemaphoreType.DMA((PIECES * len(arrays),))],
        cost_estimate=pl.CostEstimate(
            flops=0, bytes_accessed=sum(a.size * a.dtype.itemsize for a in arrays), transcendentals=0
        ),
        compiler_params=pltpu.CompilerParams(vmem_limit_bytes=16 << 20),
    )(*in_hbm(*arrays))


def second_kernel(
    section_ref, lane_ref, offset_ref, fresh_ref, gain_ref, own_ref, handed_ref, first_ref, state_ref, normed_ref
):
    tok = state_ref.shape[0]

    def block(index):
        return handed_ref[pl.ds(pl.multiple_of(index * tok, tok), tok)].astype(jnp.float32)

    odd = lane_ref[0] % 2
    first, handed = own_ref[...], block(odd)
    for index in range(2, handed_ref.shape[0] // tok, 3):
        first = first + block(index)
        handed = handed + block(index + 2 - odd)
    first_ref[...] = first.astype(jnp.bfloat16)
    picked = fresh_ref[pl.ds(pl.multiple_of(offset_ref[0] * tok, tok), tok)]
    state = jnp.where(section_ref[0] == 0, picked, handed.astype(jnp.bfloat16))
    state_ref[...] = state
    normed_ref[...] = normalized(state, gain_ref[0])


def second_entry(section, lane, offsets, fresh, gain, own, handed):
    return pl.pallas_call(
        second_kernel,
        out_shape=(pltpu.VMEM(own.shape, jnp.bfloat16),) * 3,
        in_specs=[pl.BlockSpec(memory_space=pltpu.SMEM)] * 3 + [pl.BlockSpec(memory_space=pltpu.VMEM)] * 4,
        out_specs=(pl.BlockSpec(memory_space=pltpu.VMEM),) * 3,
        compiler_params=pltpu.CompilerParams(vmem_limit_bytes=16 << 20),
    )(section, lane, offsets, fresh, gain, own, handed)


def gathered(normed):
    lanes = lax.axis_size("lane")
    towers = [[tower * lanes + 2 * k for k in range(lanes // 2)] for tower in range(2)]
    partner = [swapped(normed, d) for d in towers[1]]
    own = [swapped(normed, d) if d else normed for d in towers[0]]
    return jnp.concatenate(own, 0), jnp.concatenate(partner, 0)


def summed(state, keep, send):
    shape = state.shape
    outs = [(shape, jnp.float32)] + [(shape, jnp.bfloat16)] * (keep.shape[0] // shape[0] - 1)
    own, *others = on_chip(sum_kernel, outs, *in_vmem(state), keep, swapped(send, 1))
    return own, others


def completed(own, others):
    for k, other in enumerate(others, 1):
        own = own + swapped(other, 2 * k).astype(jnp.float32)
    return own.astype(jnp.bfloat16)


def index_of(axis):
    return jnp.reshape(lax.axis_index(axis), (1,)).astype(jnp.int32)


def shards(in_flight, fresh_batches, offsets, norm_gain, w_query, w_keyval, w_out):
    normed, state, gain = entry(in_flight[0, 0], norm_gain[0])
    tok = state.shape[0]
    normed, section, lane = lax.optimization_barrier((normed, index_of("section"), index_of("lane")))
    (wkv,) = load(w_keyval.reshape(-1, w_keyval.shape[-1]))
    own, partner = gathered(normed)
    partner, wkv = lax.optimization_barrier((partner, wkv))
    wq, wo, fresh = w_query[0, 0], w_out[0, 0], fresh_batches.reshape(-1, fresh_batches.shape[-1])
    weights = (wq, wkv, wo)
    first_sum, others = summed(state, *layer_part(own, partner, weights, tok))
    handed = handed_on(first_sum.astype(jnp.bfloat16), others)
    first, state, normed = second_entry(section, lane, offsets, fresh, gain, first_sum, handed)
    own, partner = gathered(normed)
    second = completed(*summed(state, *layer_part(own, partner, weights, tok)))
    return jnp.stack([first, second])[:, None, None]


def solution(mesh):
    placed = (
        P("section", "tower", "lane", None),
        P(None, "tower", "lane", None),
        P("lane"),
        P("section", "tower", None),
        P("section", "tower", None, "lane"),
        P("section", "tower", None, None, "lane"),
        P("section", "tower", "lane", None),
    )
    return jax.shard_map(
        shards,
        mesh=mesh,
        in_specs=placed,
        out_specs=P(None, "section", "tower", "lane", None),
        check_vma=False,
    )
```

```python
import functools

import jax
import jax.numpy as jnp
from jax import lax
from jax.experimental import pallas as pl
from jax.experimental.pallas import tpu as pltpu
from jax.sharding import PartitionSpec as P

HEAD_DIM = 128
EPSILON = 1e-06
BOTH = ("tower", "lane")
PIECES = 4


def swapped(value, mask):
    count = lax.axis_size(BOTH)
    return lax.ppermute(value, BOTH, [(i, i ^ mask) for i in range(count)])


def climbed(value, hop, climbs):
    sections, lanes = lax.axis_size("section"), lax.axis_size("lane")
    pairs = []
    for s in range(sections):
        for lane in range(lanes):
            to, target = (s + 1, lane ^ hop) if lane % 2 == climbs else (s - 1, lane)
            if not 0 <= to < sections:
                to, target = s, lane ^ 1
            pairs.append((s * lanes + lane, to * lanes + target))
    return lax.ppermute(value, ("section", "lane"), pairs)


def handed_on(own, others):
    blocks = [climbed(own, 0, 0), climbed(own, 0, 1)]
    for k, other in enumerate(others, 1):
        blocks += [swapped(other, 2 * k), climbed(other, 2 * k, 1), climbed(other, 2 * k, 0)]
    return jnp.concatenate(blocks, 0)


def in_hbm(*arrays):
    return [pltpu.with_memory_space_constraint(a, pltpu.HBM) for a in arrays]


def normalized(state, gain):
    wide = state.astype(jnp.float32)
    scale = lax.rsqrt(jnp.mean(wide * wide, -1, keepdims=True) + EPSILON)
    return (wide * scale * gain).astype(jnp.bfloat16)


def project(left, right):
    return jnp.dot(left, right, preferred_element_type=jnp.float32).astype(jnp.bfloat16)


def query_kernel(mine_ref, theirs_ref, wq_ref, query_ref):
    query_ref[...] = project(jnp.concatenate([mine_ref[...], theirs_ref[...]], 0), wq_ref[...])


def attend_kernel(tok, mine_ref, theirs_ref, query_ref, wkv_ref, wo_ref, keep_ref, send_ref):
    half, width = keep_ref.shape
    rows = 2 * half
    partner = jnp.concatenate([mine_ref[...], theirs_ref[...]], 0)
    keys = project(partner, wkv_ref[:width])
    values = project(partner, wkv_ref[width:])
    row_clip = lax.broadcasted_iota(jnp.int32, (rows, rows), 0) // tok
    col_clip = lax.broadcasted_iota(jnp.int32, (rows, rows), 1) // tok
    same_clip = row_clip == col_clip
    heads = [slice(start, start + HEAD_DIM) for start in range(0, keys.shape[1], HEAD_DIM)]
    scores = [
        lax.dot_general(
            query_ref[:, head], keys[:, head], (((1,), (1,)), ((), ())), preferred_element_type=jnp.float32
        )
        for head in heads
    ]
    scores = [jnp.where(same_clip, score * (HEAD_DIM**-0.5), -jnp.inf) for score in scores]
    tops = [jnp.max(score, -1, keepdims=True) for score in scores]
    weights = [jnp.exp(score - top).astype(jnp.bfloat16) for score, top in zip(scores, tops)]
    ones = jnp.ones((rows, HEAD_DIM), jnp.bfloat16)
    sums = [jnp.dot(weight, ones, preferred_element_type=jnp.float32) for weight in weights]
    mixed = [
        jnp.dot(weight, values[:, head], preferred_element_type=jnp.float32)
        for weight, head in zip(weights, heads)
    ]
    mixed = jnp.concatenate([(mix / total).astype(jnp.bfloat16) for mix, total in zip(mixed, sums)], 1)
    for start in range(0, width, width // 4):
        columns = slice(start, start + width // 4)
        part = jnp.dot(mixed, wo_ref[:, columns], preferred_element_type=jnp.float32)
        keep_ref[:, columns] = part[:half]
        send_ref[:, columns] = part[half:].astype(jnp.bfloat16)


def in_vmem(*arrays):
    return [pltpu.with_memory_space_constraint(a, pltpu.VMEM) for a in arrays]


def on_chip(kernel, outs, *arrays, flops=0):
    size = sum(a.size * a.dtype.itemsize for a in arrays)
    return pl.pallas_call(
        kernel,
        out_shape=tuple(jax.ShapeDtypeStruct(shape, dtype) for shape, dtype in outs),
        in_specs=[pl.BlockSpec(memory_space=pltpu.VMEM)] * len(arrays),
        out_specs=(pl.BlockSpec(memory_space=pltpu.VMEM),) * len(outs),
        cost_estimate=pl.CostEstimate(flops=flops, bytes_accessed=size, transcendentals=0),
        compiler_params=pltpu.CompilerParams(vmem_limit_bytes=16 << 20),
    )(*arrays)


def layer_part(own, partner, weights, tok):
    wq, wkv, wo = weights[0], *in_vmem(weights[1]), weights[2]
    (half, width), head_cols = own.shape, wq.shape[1]
    pushed = 2 * 256 * width * head_cols
    (query,) = on_chip(
        query_kernel, [((2 * half, head_cols), jnp.bfloat16)], own, swapped(own, 1), wq, flops=pushed
    )
    return on_chip(
        functools.partial(attend_kernel, tok),
        [((half, width), jnp.float32), ((half, width), jnp.bfloat16)],
        partner, swapped(partner, 1), query, wkv, wo,
        flops=4 * pushed,
    )


def sum_kernel(state_ref, keep_ref, sent_ref, own_ref, *out_refs):
    tok = state_ref.shape[0]
    total = keep_ref[...] + sent_ref[...].astype(jnp.float32)
    own_ref[...] = state_ref[...].astype(jnp.float32) + total[:tok]
    for k, out_ref in enumerate(out_refs, 1):
        out_ref[...] = total[k * tok : (k + 1) * tok].astype(jnp.bfloat16)


def entry_kernel(x_ref, gain_ref, normed_ref, x_out, gain_out, sems):
    width = x_ref.shape[1] // PIECES
    copies = [pltpu.make_async_copy(gain_ref, gain_out, sems.at[PIECES])]
    for i in range(PIECES):
        here = (slice(None), pl.ds(i * width, width))
        copies.append(pltpu.make_async_copy(x_ref.at[here], x_out.at[here], sems.at[i]))
    for copy in copies:
        copy.start()
    for copy in copies:
        copy.wait()
    normed_ref[...] = normalized(x_out[...], gain_out[0])


def entry(state, gain):
    return pl.pallas_call(
        entry_kernel,
        out_shape=(
            pltpu.VMEM(state.shape, jnp.bfloat16),
            pltpu.VMEM(state.shape, state.dtype),
            pltpu.VMEM(gain.shape, gain.dtype),
        ),
        in_specs=[pl.BlockSpec(memory_space=pltpu.HBM)] * 2,
        out_specs=(pl.BlockSpec(memory_space=pltpu.VMEM),) * 3,
        scratch_shapes=[pltpu.SemaphoreType.DMA((PIECES + 1,))],
        compiler_params=pltpu.CompilerParams(vmem_limit_bytes=16 << 20),
    )(*in_hbm(state, gain))


def load_kernel(*refs):
    *refs, sems = refs
    count = len(refs) // 2
    copies = []
    for source, target in zip(refs[:count], refs[count:]):
        pieces = PIECES if source.shape[0] % (16 * PIECES) == 0 else 1
        rows = source.shape[0] // pieces
        for i in range(pieces):
            here = pl.ds(i * rows, rows)
            copies.append(pltpu.make_async_copy(source.at[here], target.at[here], sems.at[len(copies)]))
            copies[-1].start()
    for copy in copies:
        copy.wait()


def load(*arrays):
    return pl.pallas_call(
        load_kernel,
        out_shape=tuple(pltpu.VMEM(a.shape, a.dtype) for a in arrays),
        in_specs=[pl.BlockSpec(memory_space=pltpu.HBM)] * len(arrays),
        out_specs=(pl.BlockSpec(memory_space=pltpu.VMEM),) * len(arrays),
        scratch_shapes=[pltpu.SemaphoreType.DMA((PIECES * len(arrays),))],
        cost_estimate=pl.CostEstimate(
            flops=0, bytes_accessed=sum(a.size * a.dtype.itemsize for a in arrays), transcendentals=0
        ),
        compiler_params=pltpu.CompilerParams(vmem_limit_bytes=16 << 20),
    )(*in_hbm(*arrays))


def second_kernel(
    section_ref, lane_ref, offset_ref, fresh_ref, gain_ref, own_ref, handed_ref, first_ref, state_ref, normed_ref
):
    tok = state_ref.shape[0]

    def block(index):
        return handed_ref[pl.ds(pl.multiple_of(index * tok, tok), tok)].astype(jnp.float32)

    odd = lane_ref[0] % 2
    first, handed = own_ref[...], block(odd)
    for index in range(2, handed_ref.shape[0] // tok, 3):
        first = first + block(index)
        handed = handed + block(index + 2 - odd)
    first_ref[...] = first.astype(jnp.bfloat16)
    picked = fresh_ref[pl.ds(pl.multiple_of(offset_ref[0] * tok, tok), tok)]
    state = jnp.where(section_ref[0] == 0, picked, handed.astype(jnp.bfloat16))
    state_ref[...] = state
    normed_ref[...] = normalized(state, gain_ref[0])


def second_entry(section, lane, offsets, fresh, gain, own, handed):
    return pl.pallas_call(
        second_kernel,
        out_shape=(pltpu.VMEM(own.shape, jnp.bfloat16),) * 3,
        in_specs=[pl.BlockSpec(memory_space=pltpu.SMEM)] * 3 + [pl.BlockSpec(memory_space=pltpu.VMEM)] * 4,
        out_specs=(pl.BlockSpec(memory_space=pltpu.VMEM),) * 3,
        compiler_params=pltpu.CompilerParams(vmem_limit_bytes=16 << 20),
    )(section, lane, offsets, fresh, gain, own, handed)


def gathered(normed):
    lanes = lax.axis_size("lane")
    towers = [[tower * lanes + 2 * k for k in range(lanes // 2)] for tower in range(2)]
    partner = [swapped(normed, d) for d in towers[1]]
    own = [swapped(normed, d) if d else normed for d in towers[0]]
    return jnp.concatenate(own, 0), jnp.concatenate(partner, 0)


def summed(state, keep, send):
    shape = state.shape
    outs = [(shape, jnp.float32)] + [(shape, jnp.bfloat16)] * (keep.shape[0] // shape[0] - 1)
    own, *others = on_chip(sum_kernel, outs, *in_vmem(state), keep, swapped(send, 1))
    return own, others


def completed(own, others):
    for k, other in enumerate(others, 1):
        own = own + swapped(other, 2 * k).astype(jnp.float32)
    return own.astype(jnp.bfloat16)


def index_of(axis):
    return jnp.reshape(lax.axis_index(axis), (1,)).astype(jnp.int32)


def shards(in_flight, fresh_batches, offsets, norm_gain, w_query, w_keyval, w_out):
    normed, state, gain = entry(in_flight[0, 0], norm_gain[0])
    tok = state.shape[0]
    normed, section, lane = lax.optimization_barrier((normed, index_of("section"), index_of("lane")))
    (wkv,) = load(w_keyval.reshape(-1, w_keyval.shape[-1]))
    own, partner = gathered(normed)
    partner, wkv = lax.optimization_barrier((partner, wkv))
    wq, wo, fresh = w_query[0, 0], w_out[0, 0], fresh_batches.reshape(-1, fresh_batches.shape[-1])
    weights = (wq, wkv, wo)
    first_sum, others = summed(state, *layer_part(own, partner, weights, tok))
    handed = handed_on(first_sum.astype(jnp.bfloat16), others)
    first, state, normed = second_entry(section, lane, offsets, fresh, gain, first_sum, handed)
    own, partner = gathered(normed)
    second = completed(*summed(state, *layer_part(own, partner, weights, tok)))
    return jnp.stack([first, second])[:, None, None]


def solution(mesh):
    placed = (
        P("section", "tower", "lane", None),
        P(None, "tower", "lane", None),
        P("lane"),
        P("section", "tower", None),
        P("section", "tower", None, "lane"),
        P("section", "tower", None, None, "lane"),
        P("section", "tower", "lane", None),
    )
    return jax.shard_map(
        shards,
        mesh=mesh,
        in_specs=placed,
        out_specs=P(None, "section", "tower", "lane", None),
        check_vma=False,
    )
```

```python
import functools

import jax
import jax.numpy as jnp
from jax import lax
from jax.experimental import pallas as pl
from jax.experimental.pallas import tpu as pltpu
from jax.sharding import PartitionSpec as P

HEAD_DIM = 128
EPSILON = 1e-06
BOTH = ("tower", "lane")
PIECES = 4


def swapped(value, mask):
    count = lax.axis_size(BOTH)
    return lax.ppermute(value, BOTH, [(i, i ^ mask) for i in range(count)])


def climbed(value, hop, climbs):
    sections, lanes = lax.axis_size("section"), lax.axis_size("lane")
    pairs = []
    for s in range(sections):
        for lane in range(lanes):
            to, target = (s + 1, lane ^ hop) if lane % 2 == climbs else (s - 1, lane)
            if not 0 <= to < sections:
                to, target = s, lane ^ 1
            pairs.append((s * lanes + lane, to * lanes + target))
    return lax.ppermute(value, ("section", "lane"), pairs)


def handed_on(own, others):
    blocks = [climbed(own, 0, 0), climbed(own, 0, 1)]
    for k, other in enumerate(others, 1):
        blocks += [climbed(other, 2 * k, 1), climbed(other, 2 * k, 0)]
    return jnp.concatenate(blocks, 0)


def in_hbm(*arrays):
    return [pltpu.with_memory_space_constraint(a, pltpu.HBM) for a in arrays]


def normalized(state, gain):
    wide = state.astype(jnp.float32)
    scale = lax.rsqrt(jnp.mean(wide * wide, -1, keepdims=True) + EPSILON)
    return (wide * scale * gain).astype(jnp.bfloat16)


def project(left, right):
    return jnp.dot(left, right, preferred_element_type=jnp.float32).astype(jnp.bfloat16)


def keyval_kernel(mine_ref, theirs_ref, wkv_ref, keys_ref, values_ref):
    depth = mine_ref.shape[1]
    partner = jnp.concatenate([mine_ref[...], theirs_ref[...]], 0)
    keys_ref[...] = project(partner, wkv_ref[:depth])
    values_ref[...] = project(partner, wkv_ref[depth:])


def attend_kernel(tok, mine_ref, theirs_ref, keys_ref, values_ref, wq_ref, wo_ref, keep_ref, send_ref):
    half, width = keep_ref.shape
    rows = 2 * half
    query = project(jnp.concatenate([mine_ref[...], theirs_ref[...]], 0), wq_ref[...])
    row_clip = lax.broadcasted_iota(jnp.int32, (rows, rows), 0) // tok
    col_clip = lax.broadcasted_iota(jnp.int32, (rows, rows), 1) // tok
    same_clip = row_clip == col_clip
    heads = [slice(start, start + HEAD_DIM) for start in range(0, query.shape[1], HEAD_DIM)]
    scores = [
        lax.dot_general(
            query[:, head], keys_ref[:, head], (((1,), (1,)), ((), ())), preferred_element_type=jnp.float32
        )
        for head in heads
    ]
    scores = [jnp.where(same_clip, score * (HEAD_DIM**-0.5), -jnp.inf) for score in scores]
    tops = [jnp.max(score, -1, keepdims=True) for score in scores]
    weights = [jnp.exp(score - top).astype(jnp.bfloat16) for score, top in zip(scores, tops)]
    ones = jnp.ones((rows, HEAD_DIM), jnp.bfloat16)
    sums = [jnp.dot(weight, ones, preferred_element_type=jnp.float32) for weight in weights]
    mixed = [
        jnp.dot(weight, values_ref[:, head], preferred_element_type=jnp.float32)
        for weight, head in zip(weights, heads)
    ]
    mixed = jnp.concatenate([(mix / total).astype(jnp.bfloat16) for mix, total in zip(mixed, sums)], 1)
    for start in range(0, width, width // 4):
        columns = slice(start, start + width // 4)
        part = jnp.dot(mixed, wo_ref[:, columns], preferred_element_type=jnp.float32)
        keep_ref[:, columns] = part[:half]
        send_ref[:, columns] = part[half:].astype(jnp.bfloat16)


def in_vmem(*arrays):
    return [pltpu.with_memory_space_constraint(a, pltpu.VMEM) for a in arrays]


def on_chip(kernel, outs, *arrays, flops=0):
    size = sum(a.size * a.dtype.itemsize for a in arrays)
    return pl.pallas_call(
        kernel,
        out_shape=tuple(jax.ShapeDtypeStruct(shape, dtype) for shape, dtype in outs),
        in_specs=[pl.BlockSpec(memory_space=pltpu.VMEM)] * len(arrays),
        out_specs=(pl.BlockSpec(memory_space=pltpu.VMEM),) * len(outs),
        cost_estimate=pl.CostEstimate(flops=flops, bytes_accessed=size, transcendentals=0),
        compiler_params=pltpu.CompilerParams(vmem_limit_bytes=16 << 20),
    )(*arrays)


def layer_part(own, partner, weights, tok, beside=()):
    wq, wkv, wo = weights[0], *in_vmem(weights[1]), weights[2]
    (half, width), head_cols = own.shape, wq.shape[1]
    partner_theirs = swapped(partner, 1)
    own_theirs = swapped(own, 1)
    if beside:
        partner_theirs, *beside = lax.optimization_barrier((partner_theirs, *beside))
    pushed = 2 * 256 * width * head_cols
    keys, values = on_chip(
        keyval_kernel,
        [((2 * half, head_cols), jnp.bfloat16)] * 2,
        partner, partner_theirs, wkv,
        flops=2 * pushed,
    )
    keep, send = on_chip(
        functools.partial(attend_kernel, tok),
        [((half, width), jnp.float32), ((half, width), jnp.bfloat16)],
        own, own_theirs, keys, values, wq, wo,
        flops=3 * pushed,
    )
    return keep, send, beside


def sum_kernel(state_ref, keep_ref, sent_ref, own_ref, *out_refs):
    tok = state_ref.shape[0]
    total = keep_ref[...] + sent_ref[...].astype(jnp.float32)
    own_ref[...] = state_ref[...].astype(jnp.float32) + total[-tok:]
    for k, out_ref in enumerate(out_refs, 1):
        start = total.shape[0] - (k + 1) * tok
        out_ref[...] = total[start : start + tok].astype(jnp.bfloat16)


def entry_kernel(x_ref, gain_ref, normed_ref, x_out, gain_out, sems):
    width = x_ref.shape[1] // PIECES
    copies = [pltpu.make_async_copy(gain_ref, gain_out, sems.at[PIECES])]
    for i in range(PIECES):
        here = (slice(None), pl.ds(i * width, width))
        copies.append(pltpu.make_async_copy(x_ref.at[here], x_out.at[here], sems.at[i]))
    for copy in copies:
        copy.start()
    for copy in copies:
        copy.wait()
    normed_ref[...] = normalized(x_out[...], gain_out[0])


def entry(state, gain):
    return pl.pallas_call(
        entry_kernel,
        out_shape=(
            pltpu.VMEM(state.shape, jnp.bfloat16),
            pltpu.VMEM(state.shape, state.dtype),
            pltpu.VMEM(gain.shape, gain.dtype),
        ),
        in_specs=[pl.BlockSpec(memory_space=pltpu.HBM)] * 2,
        out_specs=(pl.BlockSpec(memory_space=pltpu.VMEM),) * 3,
        scratch_shapes=[pltpu.SemaphoreType.DMA((PIECES + 1,))],
        compiler_params=pltpu.CompilerParams(vmem_limit_bytes=16 << 20),
    )(*in_hbm(state, gain))


def load_kernel(*refs):
    *refs, sems = refs
    count = len(refs) // 2
    copies = []
    for source, target in zip(refs[:count], refs[count:]):
        pieces = PIECES if source.shape[0] % (16 * PIECES) == 0 else 1
        rows = source.shape[0] // pieces
        for i in range(pieces):
            here = pl.ds(i * rows, rows)
            copies.append(pltpu.make_async_copy(source.at[here], target.at[here], sems.at[len(copies)]))
            copies[-1].start()
    for copy in copies:
        copy.wait()


def load(*arrays):
    return pl.pallas_call(
        load_kernel,
        out_shape=tuple(pltpu.VMEM(a.shape, a.dtype) for a in arrays),
        in_specs=[pl.BlockSpec(memory_space=pltpu.HBM)] * len(arrays),
        out_specs=(pl.BlockSpec(memory_space=pltpu.VMEM),) * len(arrays),
        scratch_shapes=[pltpu.SemaphoreType.DMA((PIECES * len(arrays),))],
        cost_estimate=pl.CostEstimate(
            flops=0, bytes_accessed=sum(a.size * a.dtype.itemsize for a in arrays), transcendentals=0
        ),
        compiler_params=pltpu.CompilerParams(vmem_limit_bytes=16 << 20),
    )(*in_hbm(*arrays))


def second_kernel(section_ref, lane_ref, offset_ref, fresh_ref, gain_ref, handed_ref, state_ref, normed_ref):
    tok = state_ref.shape[0]

    def block(index):
        return handed_ref[pl.ds(pl.multiple_of(index * tok, tok), tok)].astype(jnp.float32)

    odd = lane_ref[0] % 2
    handed = block(odd)
    for index in range(2, handed_ref.shape[0] // tok, 2):
        handed = handed + block(index + 1 - odd)
    picked = fresh_ref[pl.ds(pl.multiple_of(offset_ref[0] * tok, tok), tok)]
    state = jnp.where(section_ref[0] == 0, picked, handed.astype(jnp.bfloat16))
    state_ref[...] = state
    normed_ref[...] = normalized(state, gain_ref[0])


def second_entry(section, lane, offsets, fresh, gain, handed, tok):
    shape = (tok, handed.shape[1])
    return pl.pallas_call(
        second_kernel,
        out_shape=(pltpu.VMEM(shape, jnp.bfloat16),) * 2,
        in_specs=[pl.BlockSpec(memory_space=pltpu.SMEM)] * 3 + [pl.BlockSpec(memory_space=pltpu.VMEM)] * 3,
        out_specs=(pl.BlockSpec(memory_space=pltpu.VMEM),) * 2,
        compiler_params=pltpu.CompilerParams(vmem_limit_bytes=16 << 20),
    )(section, lane, offsets, fresh, gain, handed)


def gathered(normed):
    lanes = lax.axis_size("lane")
    towers = [[tower * lanes + 2 * k for k in reversed(range(lanes // 2))] for tower in range(2)]
    partner = [swapped(normed, d) for d in towers[1]]
    own = [swapped(normed, d) if d else normed for d in towers[0]]
    return jnp.concatenate(own, 0), jnp.concatenate(partner, 0)


def summed(state, keep, send):
    shape = state.shape
    outs = [(shape, jnp.float32)] + [(shape, jnp.bfloat16)] * (keep.shape[0] // shape[0] - 1)
    own, *others = on_chip(sum_kernel, outs, *in_vmem(state), keep, swapped(send, 1))
    return own, others


def completed(own, others):
    for k, other in enumerate(others, 1):
        own = own + swapped(other, 2 * k).astype(jnp.float32)
    return own.astype(jnp.bfloat16)


def index_of(axis):
    return jnp.reshape(lax.axis_index(axis), (1,)).astype(jnp.int32)


def shards(in_flight, fresh_batches, offsets, norm_gain, w_query, w_keyval, w_out):
    normed, state, gain = entry(in_flight[0, 0], norm_gain[0])
    tok = state.shape[0]
    normed, section, lane = lax.optimization_barrier((normed, index_of("section"), index_of("lane")))
    (wkv,) = load(w_keyval.reshape(-1, w_keyval.shape[-1]))
    own, partner = gathered(normed)
    partner, wkv = lax.optimization_barrier((partner, wkv))
    wq, wo, fresh = w_query[0, 0], w_out[0, 0], fresh_batches.reshape(-1, fresh_batches.shape[-1])
    weights = (wq, wkv, wo)
    first_sum, others = summed(state, *layer_part(own, partner, weights, tok)[:2])
    handed = handed_on(first_sum.astype(jnp.bfloat16), others)
    state, normed = second_entry(section, lane, offsets, fresh, gain, handed, tok)
    normed, others = lax.optimization_barrier((normed, others))
    own, partner = gathered(normed)
    arrived = [swapped(other, 2 * k) for k, other in enumerate(others, 1)]
    keep, send, arrived = layer_part(own, partner, weights, tok, arrived)
    first = sum([rows.astype(jnp.float32) for rows in arrived], first_sum).astype(jnp.bfloat16)
    second = completed(*summed(state, keep, send))
    return jnp.stack([first, second])[:, None, None]


def solution(mesh):
    placed = (
        P("section", "tower", "lane", None),
        P(None, "tower", "lane", None),
        P("lane"),
        P("section", "tower", None),
        P("section", "tower", None, "lane"),
        P("section", "tower", None, None, "lane"),
        P("section", "tower", "lane", None),
    )
    return jax.shard_map(
        shards,
        mesh=mesh,
        in_specs=placed,
        out_specs=P(None, "section", "tower", "lane", None),
        check_vma=False,
    )
```

```python
import functools

import jax
import jax.numpy as jnp
from jax import lax
from jax.experimental import pallas as pl
from jax.experimental.pallas import tpu as pltpu
from jax.sharding import PartitionSpec as P

HEAD_DIM = 128
EPSILON = 1e-06
BOTH = ("tower", "lane")
PIECES = 4


def swapped(value, mask):
    count = lax.axis_size(BOTH)
    return lax.ppermute(value, BOTH, [(i, i ^ mask) for i in range(count)])


def climbed(value, hop, climbs):
    sections, lanes = lax.axis_size("section"), lax.axis_size("lane")
    pairs = []
    for s in range(sections):
        for lane in range(lanes):
            to, target = (s + 1, lane ^ hop) if lane % 2 == climbs else (s - 1, lane)
            if not 0 <= to < sections:
                to, target = s, lane ^ 1
            pairs.append((s * lanes + lane, to * lanes + target))
    return lax.ppermute(value, ("section", "lane"), pairs)


def handed_on(own, others):
    sums = [own, *others]
    turns = [(k, (k + turn) % 2) for turn in range(2) for k in range(len(sums))]
    return jnp.concatenate([climbed(sums[k], 2 * k, climbs) for k, climbs in turns], 0)


def in_hbm(*arrays):
    return [pltpu.with_memory_space_constraint(a, pltpu.HBM) for a in arrays]


def normalized(state, gain):
    wide = state.astype(jnp.float32)
    scale = lax.rsqrt(jnp.mean(wide * wide, -1, keepdims=True) + EPSILON)
    return (wide * scale * gain).astype(jnp.bfloat16)


def project(left, right):
    return jnp.dot(left, right, preferred_element_type=jnp.float32).astype(jnp.bfloat16)


def keyval_kernel(mine_ref, theirs_ref, wkv_ref, keys_ref, values_ref):
    depth = mine_ref.shape[1]
    partner = jnp.concatenate([mine_ref[...], theirs_ref[...]], 0)
    keys_ref[...] = project(partner, wkv_ref[:depth])
    values_ref[...] = project(partner, wkv_ref[depth:])


def attend_kernel(tok, mine_ref, theirs_ref, keys_ref, values_ref, wq_ref, wo_ref, keep_ref, send_ref):
    half, width = keep_ref.shape
    rows = 2 * half
    query = project(jnp.concatenate([mine_ref[...], theirs_ref[...]], 0), wq_ref[...])
    row_clip = lax.broadcasted_iota(jnp.int32, (rows, rows), 0) // tok
    col_clip = lax.broadcasted_iota(jnp.int32, (rows, rows), 1) // tok
    same_clip = row_clip == col_clip
    heads = [slice(start, start + HEAD_DIM) for start in range(0, query.shape[1], HEAD_DIM)]
    scores = [
        lax.dot_general(
            query[:, head], keys_ref[:, head], (((1,), (1,)), ((), ())), preferred_element_type=jnp.float32
        )
        for head in heads
    ]
    scores = [jnp.where(same_clip, score * (HEAD_DIM**-0.5), -jnp.inf) for score in scores]
    tops = [jnp.max(score, -1, keepdims=True) for score in scores]
    weights = [jnp.exp(score - top).astype(jnp.bfloat16) for score, top in zip(scores, tops)]
    ones = jnp.ones((rows, HEAD_DIM), jnp.bfloat16)
    sums = [jnp.dot(weight, ones, preferred_element_type=jnp.float32) for weight in weights]
    mixed = [
        jnp.dot(weight, values_ref[:, head], preferred_element_type=jnp.float32)
        for weight, head in zip(weights, heads)
    ]
    mixed = jnp.concatenate([(mix / total).astype(jnp.bfloat16) for mix, total in zip(mixed, sums)], 1)
    for start in range(0, width, width // 4):
        columns = slice(start, start + width // 4)
        part = jnp.dot(mixed, wo_ref[:, columns], preferred_element_type=jnp.float32)
        keep_ref[:, columns] = part[:half]
        send_ref[:, columns] = part[half:].astype(jnp.bfloat16)


def in_vmem(*arrays):
    return [pltpu.with_memory_space_constraint(a, pltpu.VMEM) for a in arrays]


def on_chip(kernel, outs, *arrays, flops=0):
    size = sum(a.size * a.dtype.itemsize for a in arrays)
    return pl.pallas_call(
        kernel,
        out_shape=tuple(jax.ShapeDtypeStruct(shape, dtype) for shape, dtype in outs),
        in_specs=[pl.BlockSpec(memory_space=pltpu.VMEM)] * len(arrays),
        out_specs=(pl.BlockSpec(memory_space=pltpu.VMEM),) * len(outs),
        cost_estimate=pl.CostEstimate(flops=flops, bytes_accessed=size, transcendentals=0),
        compiler_params=pltpu.CompilerParams(vmem_limit_bytes=16 << 20),
    )(*arrays)


def layer_part(own, partner, weights, tok, beside=()):
    wq, wkv, wo = weights[0], *in_vmem(weights[1]), weights[2]
    (half, width), head_cols = own.shape, wq.shape[1]
    partner_theirs = swapped(partner, 1)
    own_theirs = swapped(own, 1)
    if beside:
        partner_theirs, *beside = lax.optimization_barrier((partner_theirs, *beside))
    pushed = 2 * 256 * width * head_cols
    keys, values = on_chip(
        keyval_kernel,
        [((2 * half, head_cols), jnp.bfloat16)] * 2,
        partner, partner_theirs, wkv,
        flops=2 * pushed,
    )
    keep, send = on_chip(
        functools.partial(attend_kernel, tok),
        [((half, width), jnp.float32), ((half, width), jnp.bfloat16)],
        own, own_theirs, keys, values, wq, wo,
        flops=3 * pushed,
    )
    return keep, send, beside


def sum_kernel(state_ref, keep_ref, sent_ref, own_ref, *out_refs):
    tok = state_ref.shape[0]
    total = keep_ref[...] + sent_ref[...].astype(jnp.float32)
    own_ref[...] = state_ref[...].astype(jnp.float32) + total[-tok:]
    for k, out_ref in enumerate(out_refs, 1):
        start = total.shape[0] - (k + 1) * tok
        out_ref[...] = total[start : start + tok].astype(jnp.bfloat16)


def entry_kernel(x_ref, gain_ref, normed_ref, x_out, gain_out, sems):
    width = x_ref.shape[1] // PIECES
    copies = [pltpu.make_async_copy(gain_ref, gain_out, sems.at[PIECES])]
    for i in range(PIECES):
        here = (slice(None), pl.ds(i * width, width))
        copies.append(pltpu.make_async_copy(x_ref.at[here], x_out.at[here], sems.at[i]))
    for copy in copies:
        copy.start()
    for copy in copies:
        copy.wait()
    normed_ref[...] = normalized(x_out[...], gain_out[0])


def entry(state, gain):
    return pl.pallas_call(
        entry_kernel,
        out_shape=(
            pltpu.VMEM(state.shape, jnp.bfloat16),
            pltpu.VMEM(state.shape, state.dtype),
            pltpu.VMEM(gain.shape, gain.dtype),
        ),
        in_specs=[pl.BlockSpec(memory_space=pltpu.HBM)] * 2,
        out_specs=(pl.BlockSpec(memory_space=pltpu.VMEM),) * 3,
        scratch_shapes=[pltpu.SemaphoreType.DMA((PIECES + 1,))],
        compiler_params=pltpu.CompilerParams(vmem_limit_bytes=16 << 20),
    )(*in_hbm(state, gain))


def load_kernel(*refs):
    *refs, sems = refs
    count = len(refs) // 2
    copies = []
    for source, target in zip(refs[:count], refs[count:]):
        pieces = PIECES if source.shape[0] % (16 * PIECES) == 0 else 1
        rows = source.shape[0] // pieces
        for i in range(pieces):
            here = pl.ds(i * rows, rows)
            copies.append(pltpu.make_async_copy(source.at[here], target.at[here], sems.at[len(copies)]))
            copies[-1].start()
    for copy in copies:
        copy.wait()


def load(*arrays):
    return pl.pallas_call(
        load_kernel,
        out_shape=tuple(pltpu.VMEM(a.shape, a.dtype) for a in arrays),
        in_specs=[pl.BlockSpec(memory_space=pltpu.HBM)] * len(arrays),
        out_specs=(pl.BlockSpec(memory_space=pltpu.VMEM),) * len(arrays),
        scratch_shapes=[pltpu.SemaphoreType.DMA((PIECES * len(arrays),))],
        cost_estimate=pl.CostEstimate(
            flops=0, bytes_accessed=sum(a.size * a.dtype.itemsize for a in arrays), transcendentals=0
        ),
        compiler_params=pltpu.CompilerParams(vmem_limit_bytes=16 << 20),
    )(*in_hbm(*arrays))


def second_kernel(section_ref, lane_ref, offset_ref, fresh_ref, gain_ref, handed_ref, state_ref, normed_ref):
    tok = state_ref.shape[0]

    def block(index):
        return handed_ref[pl.ds(pl.multiple_of(index * tok, tok), tok)].astype(jnp.float32)

    odd = lane_ref[0] % 2
    count = handed_ref.shape[0] // (2 * tok)
    handed = 0.0
    for k in range(count):
        handed = handed + block((k + odd) % 2 * count + k)
    picked = fresh_ref[pl.ds(pl.multiple_of(offset_ref[0] * tok, tok), tok)]
    state = jnp.where(section_ref[0] == 0, picked, handed.astype(jnp.bfloat16))
    state_ref[...] = state
    normed_ref[...] = normalized(state, gain_ref[0])


def second_entry(section, lane, offsets, fresh, gain, handed, tok):
    shape = (tok, handed.shape[1])
    return pl.pallas_call(
        second_kernel,
        out_shape=(pltpu.VMEM(shape, jnp.bfloat16),) * 2,
        in_specs=[pl.BlockSpec(memory_space=pltpu.SMEM)] * 3 + [pl.BlockSpec(memory_space=pltpu.VMEM)] * 3,
        out_specs=(pl.BlockSpec(memory_space=pltpu.VMEM),) * 2,
        compiler_params=pltpu.CompilerParams(vmem_limit_bytes=16 << 20),
    )(section, lane, offsets, fresh, gain, handed)


def gathered(normed):
    lanes = lax.axis_size("lane")
    towers = [[tower * lanes + 2 * k for k in reversed(range(lanes // 2))] for tower in range(2)]
    partner = [swapped(normed, d) for d in towers[1]]
    own = [swapped(normed, d) if d else normed for d in towers[0]]
    return jnp.concatenate(own, 0), jnp.concatenate(partner, 0)


def summed(state, keep, send):
    shape = state.shape
    outs = [(shape, jnp.float32)] + [(shape, jnp.bfloat16)] * (keep.shape[0] // shape[0] - 1)
    own, *others = on_chip(sum_kernel, outs, *in_vmem(state), keep, swapped(send, 1))
    return own, others


def completed(own, others):
    for k, other in enumerate(others, 1):
        own = own + swapped(other, 2 * k).astype(jnp.float32)
    return own.astype(jnp.bfloat16)


def index_of(axis):
    return jnp.reshape(lax.axis_index(axis), (1,)).astype(jnp.int32)


def shards(in_flight, fresh_batches, offsets, norm_gain, w_query, w_keyval, w_out):
    normed, state, gain = entry(in_flight[0, 0], norm_gain[0])
    tok = state.shape[0]
    normed, section, lane = lax.optimization_barrier((normed, index_of("section"), index_of("lane")))
    (wkv,) = load(w_keyval.reshape(-1, w_keyval.shape[-1]))
    own, partner = gathered(normed)
    partner, wkv = lax.optimization_barrier((partner, wkv))
    wq, wo, fresh = w_query[0, 0], w_out[0, 0], fresh_batches.reshape(-1, fresh_batches.shape[-1])
    weights = (wq, wkv, wo)
    first_sum, others = summed(state, *layer_part(own, partner, weights, tok)[:2])
    handed = handed_on(first_sum.astype(jnp.bfloat16), others)
    state, normed = second_entry(section, lane, offsets, fresh, gain, handed, tok)
    normed, others = lax.optimization_barrier((normed, others))
    own, partner = gathered(normed)
    arrived = [swapped(other, 2 * k) for k, other in enumerate(others, 1)]
    keep, send, arrived = layer_part(own, partner, weights, tok, arrived)
    first = sum([rows.astype(jnp.float32) for rows in arrived], first_sum).astype(jnp.bfloat16)
    second = completed(*summed(state, keep, send))
    return jnp.stack([first, second])[:, None, None]


def solution(mesh):
    placed = (
        P("section", "tower", "lane", None),
        P(None, "tower", "lane", None),
        P("lane"),
        P("section", "tower", None),
        P("section", "tower", None, "lane"),
        P("section", "tower", None, None, "lane"),
        P("section", "tower", "lane", None),
    )
    return jax.shard_map(
        shards,
        mesh=mesh,
        in_specs=placed,
        out_specs=P(None, "section", "tower", "lane", None),
        check_vma=False,
    )
```

```python
import functools

import jax
import jax.numpy as jnp
from jax import lax
from jax.experimental import pallas as pl
from jax.experimental.pallas import tpu as pltpu
from jax.sharding import PartitionSpec as P

HEAD_DIM = 128
EPSILON = 1e-06
BOTH = ("tower", "lane")
PIECES = 4


def swapped(value, mask):
    count = lax.axis_size(BOTH)
    return lax.ppermute(value, BOTH, [(i, i ^ mask) for i in range(count)])


def climbed(value, hop, climbs):
    sections, lanes = lax.axis_size("section"), lax.axis_size("lane")
    pairs = []
    for s in range(sections):
        for lane in range(lanes):
            to, target = (s + 1, lane ^ hop) if lane % 2 == climbs else (s - 1, lane)
            if not 0 <= to < sections:
                to, target = s, lane ^ 1
            pairs.append((s * lanes + lane, to * lanes + target))
    return lax.ppermute(value, ("section", "lane"), pairs)


def handed_on(own, others):
    sums = [own, *others]
    turns = [(k, (k + turn) % 2) for turn in range(2) for k in range(len(sums))]
    return jnp.concatenate([climbed(sums[k], 2 * k, climbs) for k, climbs in turns], 0)


def in_hbm(*arrays):
    return [pltpu.with_memory_space_constraint(a, pltpu.HBM) for a in arrays]


def normalized(state, gain):
    wide = state.astype(jnp.float32)
    scale = lax.rsqrt(jnp.mean(wide * wide, -1, keepdims=True) + EPSILON)
    return (wide * scale * gain).astype(jnp.bfloat16)


def project(left, right):
    return jnp.dot(left, right, preferred_element_type=jnp.float32).astype(jnp.bfloat16)


def keyval_kernel(mine_ref, theirs_ref, wkv_ref, keys_ref, values_ref):
    depth = mine_ref.shape[1]
    partner = jnp.concatenate([mine_ref[...], theirs_ref[...]], 0)
    keys_ref[...] = project(partner, wkv_ref[:depth])
    values_ref[...] = project(partner, wkv_ref[depth:])


def attend_kernel(tok, mine_ref, theirs_ref, keys_ref, values_ref, wq_ref, wo_ref, keep_ref, send_ref):
    half, width = keep_ref.shape
    rows = 2 * half
    query = project(jnp.concatenate([mine_ref[...], theirs_ref[...]], 0), wq_ref[...])
    row_clip = lax.broadcasted_iota(jnp.int32, (rows, rows), 0) // tok
    col_clip = lax.broadcasted_iota(jnp.int32, (rows, rows), 1) // tok
    same_clip = row_clip == col_clip
    heads = [slice(start, start + HEAD_DIM) for start in range(0, query.shape[1], HEAD_DIM)]
    scores = [
        lax.dot_general(
            query[:, head], keys_ref[:, head], (((1,), (1,)), ((), ())), preferred_element_type=jnp.float32
        )
        for head in heads
    ]
    scores = [jnp.where(same_clip, score * (HEAD_DIM**-0.5), -jnp.inf) for score in scores]
    tops = [jnp.max(score, -1, keepdims=True) for score in scores]
    weights = [jnp.exp(score - top).astype(jnp.bfloat16) for score, top in zip(scores, tops)]
    ones = jnp.ones((rows, HEAD_DIM), jnp.bfloat16)
    sums = [jnp.dot(weight, ones, preferred_element_type=jnp.float32) for weight in weights]
    mixed = [
        jnp.dot(weight, values_ref[:, head], preferred_element_type=jnp.float32)
        for weight, head in zip(weights, heads)
    ]
    mixed = jnp.concatenate([(mix / total).astype(jnp.bfloat16) for mix, total in zip(mixed, sums)], 1)
    for start in range(0, width, width // 2):
        columns = slice(start, start + width // 2)
        part = jnp.dot(mixed, wo_ref[:, columns], preferred_element_type=jnp.float32)
        keep_ref[:, columns] = part[:half]
        send_ref[:, columns] = part[half:].astype(jnp.bfloat16)


def in_vmem(*arrays):
    return [pltpu.with_memory_space_constraint(a, pltpu.VMEM) for a in arrays]


def on_chip(kernel, outs, *arrays, flops=0):
    size = sum(a.size * a.dtype.itemsize for a in arrays)
    return pl.pallas_call(
        kernel,
        out_shape=tuple(jax.ShapeDtypeStruct(shape, dtype) for shape, dtype in outs),
        in_specs=[pl.BlockSpec(memory_space=pltpu.VMEM)] * len(arrays),
        out_specs=(pl.BlockSpec(memory_space=pltpu.VMEM),) * len(outs),
        cost_estimate=pl.CostEstimate(flops=flops, bytes_accessed=size, transcendentals=0),
        compiler_params=pltpu.CompilerParams(vmem_limit_bytes=16 << 20),
    )(*arrays)


def layer_part(own, partner, weights, tok, beside=()):
    wq, wkv, wo = weights[0], *in_vmem(weights[1]), weights[2]
    (half, width), head_cols = own.shape, wq.shape[1]
    partner_theirs = swapped(partner, 1)
    own_theirs = swapped(own, 1)
    if beside:
        partner_theirs, *beside = lax.optimization_barrier((partner_theirs, *beside))
    pushed = 2 * 256 * width * head_cols
    keys, values = on_chip(
        keyval_kernel,
        [((2 * half, head_cols), jnp.bfloat16)] * 2,
        partner, partner_theirs, wkv,
        flops=2 * pushed,
    )
    keep, send = on_chip(
        functools.partial(attend_kernel, tok),
        [((half, width), jnp.float32), ((half, width), jnp.bfloat16)],
        own, own_theirs, keys, values, wq, wo,
        flops=3 * pushed,
    )
    return keep, send, beside


def sum_kernel(state_ref, keep_ref, sent_ref, own_ref, *out_refs):
    tok = state_ref.shape[0]
    total = keep_ref[...] + sent_ref[...].astype(jnp.float32)
    own_ref[...] = state_ref[...].astype(jnp.float32) + total[-tok:]
    for k, out_ref in enumerate(out_refs, 1):
        start = total.shape[0] - (k + 1) * tok
        out_ref[...] = total[start : start + tok].astype(jnp.bfloat16)


def entry_kernel(x_ref, gain_ref, normed_ref, x_out, gain_out, sems):
    width = x_ref.shape[1] // PIECES
    copies = [pltpu.make_async_copy(gain_ref, gain_out, sems.at[PIECES])]
    for i in range(PIECES):
        here = (slice(None), pl.ds(i * width, width))
        copies.append(pltpu.make_async_copy(x_ref.at[here], x_out.at[here], sems.at[i]))
    for copy in copies:
        copy.start()
    for copy in copies:
        copy.wait()
    normed_ref[...] = normalized(x_out[...], gain_out[0])


def entry(state, gain):
    return pl.pallas_call(
        entry_kernel,
        out_shape=(
            pltpu.VMEM(state.shape, jnp.bfloat16),
            pltpu.VMEM(state.shape, state.dtype),
            pltpu.VMEM(gain.shape, gain.dtype),
        ),
        in_specs=[pl.BlockSpec(memory_space=pltpu.HBM)] * 2,
        out_specs=(pl.BlockSpec(memory_space=pltpu.VMEM),) * 3,
        scratch_shapes=[pltpu.SemaphoreType.DMA((PIECES + 1,))],
        compiler_params=pltpu.CompilerParams(vmem_limit_bytes=16 << 20),
    )(*in_hbm(state, gain))


def load_kernel(*refs):
    *refs, sems = refs
    count = len(refs) // 2
    copies = []
    for source, target in zip(refs[:count], refs[count:]):
        pieces = PIECES if source.shape[0] % (16 * PIECES) == 0 else 1
        rows = source.shape[0] // pieces
        for i in range(pieces):
            here = pl.ds(i * rows, rows)
            copies.append(pltpu.make_async_copy(source.at[here], target.at[here], sems.at[len(copies)]))
            copies[-1].start()
    for copy in copies:
        copy.wait()


def load(*arrays):
    return pl.pallas_call(
        load_kernel,
        out_shape=tuple(pltpu.VMEM(a.shape, a.dtype) for a in arrays),
        in_specs=[pl.BlockSpec(memory_space=pltpu.HBM)] * len(arrays),
        out_specs=(pl.BlockSpec(memory_space=pltpu.VMEM),) * len(arrays),
        scratch_shapes=[pltpu.SemaphoreType.DMA((PIECES * len(arrays),))],
        cost_estimate=pl.CostEstimate(
            flops=0, bytes_accessed=sum(a.size * a.dtype.itemsize for a in arrays), transcendentals=0
        ),
        compiler_params=pltpu.CompilerParams(vmem_limit_bytes=16 << 20),
    )(*in_hbm(*arrays))


def second_kernel(section_ref, lane_ref, offset_ref, fresh_ref, gain_ref, handed_ref, state_ref, normed_ref):
    tok = state_ref.shape[0]

    def block(index):
        return handed_ref[pl.ds(pl.multiple_of(index * tok, tok), tok)].astype(jnp.float32)

    odd = lane_ref[0] % 2
    count = handed_ref.shape[0] // (2 * tok)
    handed = 0.0
    for k in range(count):
        handed = handed + block((k + odd) % 2 * count + k)
    picked = fresh_ref[pl.ds(pl.multiple_of(offset_ref[0] * tok, tok), tok)]
    state = jnp.where(section_ref[0] == 0, picked, handed.astype(jnp.bfloat16))
    state_ref[...] = state
    normed_ref[...] = normalized(state, gain_ref[0])


def second_entry(section, lane, offsets, fresh, gain, handed, tok):
    shape = (tok, handed.shape[1])
    return pl.pallas_call(
        second_kernel,
        out_shape=(pltpu.VMEM(shape, jnp.bfloat16),) * 2,
        in_specs=[pl.BlockSpec(memory_space=pltpu.SMEM)] * 3 + [pl.BlockSpec(memory_space=pltpu.VMEM)] * 3,
        out_specs=(pl.BlockSpec(memory_space=pltpu.VMEM),) * 2,
        compiler_params=pltpu.CompilerParams(vmem_limit_bytes=16 << 20),
    )(section, lane, offsets, fresh, gain, handed)


def gathered(normed):
    lanes = lax.axis_size("lane")
    towers = [[tower * lanes + 2 * k for k in reversed(range(lanes // 2))] for tower in range(2)]
    partner = [swapped(normed, d) for d in towers[1]]
    own = [swapped(normed, d) if d else normed for d in towers[0]]
    return jnp.concatenate(own, 0), jnp.concatenate(partner, 0)


def summed(state, keep, send):
    shape = state.shape
    outs = [(shape, jnp.float32)] + [(shape, jnp.bfloat16)] * (keep.shape[0] // shape[0] - 1)
    own, *others = on_chip(sum_kernel, outs, *in_vmem(state), keep, swapped(send, 1))
    return own, others


def completed(own, others):
    for k, other in enumerate(others, 1):
        own = own + swapped(other, 2 * k).astype(jnp.float32)
    return own.astype(jnp.bfloat16)


def index_of(axis):
    return jnp.reshape(lax.axis_index(axis), (1,)).astype(jnp.int32)


def shards(in_flight, fresh_batches, offsets, norm_gain, w_query, w_keyval, w_out):
    normed, state, gain = entry(in_flight[0, 0], norm_gain[0])
    tok = state.shape[0]
    normed, section, lane = lax.optimization_barrier((normed, index_of("section"), index_of("lane")))
    (wkv,) = load(w_keyval.reshape(-1, w_keyval.shape[-1]))
    own, partner = gathered(normed)
    partner, wkv = lax.optimization_barrier((partner, wkv))
    wq, wo, fresh = w_query[0, 0], w_out[0, 0], fresh_batches.reshape(-1, fresh_batches.shape[-1])
    weights = (wq, wkv, wo)
    first_sum, others = summed(state, *layer_part(own, partner, weights, tok)[:2])
    handed = handed_on(first_sum.astype(jnp.bfloat16), others)
    state, normed = second_entry(section, lane, offsets, fresh, gain, handed, tok)
    normed, others = lax.optimization_barrier((normed, others))
    own, partner = gathered(normed)
    arrived = [swapped(other, 2 * k) for k, other in enumerate(others, 1)]
    keep, send, arrived = layer_part(own, partner, weights, tok, arrived)
    first = sum([rows.astype(jnp.float32) for rows in arrived], first_sum).astype(jnp.bfloat16)
    second = completed(*summed(state, keep, send))
    return jnp.stack([first, second])[:, None, None]


def solution(mesh):
    placed = (
        P("section", "tower", "lane", None),
        P(None, "tower", "lane", None),
        P("lane"),
        P("section", "tower", None),
        P("section", "tower", None, "lane"),
        P("section", "tower", None, None, "lane"),
        P("section", "tower", "lane", None),
    )
    return jax.shard_map(
        shards,
        mesh=mesh,
        in_specs=placed,
        out_specs=P(None, "section", "tower", "lane", None),
        check_vma=False,
    )
```

```python
import functools

import jax
import jax.numpy as jnp
from jax import lax
from jax.experimental import pallas as pl
from jax.experimental.pallas import tpu as pltpu
from jax.sharding import PartitionSpec as P

HEAD_DIM = 128
EPSILON = 1e-06
BOTH = ("tower", "lane")
PIECES = 4


def swapped(value, mask):
    count = lax.axis_size(BOTH)
    return lax.ppermute(value, BOTH, [(i, i ^ mask) for i in range(count)])


def climbed(value, hop, climbs):
    sections, lanes = lax.axis_size("section"), lax.axis_size("lane")
    pairs = []
    for s in range(sections):
        for lane in range(lanes):
            to, target = (s + 1, lane ^ hop) if lane % 2 == climbs else (s - 1, lane)
            if not 0 <= to < sections:
                to, target = s, lane ^ 1
            pairs.append((s * lanes + lane, to * lanes + target))
    return lax.ppermute(value, ("section", "lane"), pairs)


def handed_on(own, others):
    sums = [own, *others]
    turns = [(k, (k + turn) % 2) for turn in range(2) for k in range(len(sums))]
    return jnp.concatenate([climbed(sums[k], 2 * k, climbs) for k, climbs in turns], 0)


def in_hbm(*arrays):
    return [pltpu.with_memory_space_constraint(a, pltpu.HBM) for a in arrays]


def normalized(state, gain):
    wide = state.astype(jnp.float32)
    scale = lax.rsqrt(jnp.mean(wide * wide, -1, keepdims=True) + EPSILON)
    return (wide * scale * gain).astype(jnp.bfloat16)


def project(left, right):
    return jnp.dot(left, right, preferred_element_type=jnp.float32).astype(jnp.bfloat16)


def keyval_kernel(mine_ref, theirs_ref, wkv_ref, keys_ref, values_ref):
    depth = mine_ref.shape[1]
    partner = jnp.concatenate([mine_ref[...], theirs_ref[...]], 0)
    keys_ref[...] = project(partner, wkv_ref[:depth])
    values_ref[...] = project(partner, wkv_ref[depth:])


def attend_kernel(tok, mine_ref, theirs_ref, keys_ref, values_ref, wq_ref, wo_ref, keep_ref, send_ref):
    half, width = keep_ref.shape
    rows = 2 * half
    query = project(jnp.concatenate([mine_ref[...], theirs_ref[...]], 0), wq_ref[...])
    row_clip = lax.broadcasted_iota(jnp.int32, (rows, rows), 0) // tok
    col_clip = lax.broadcasted_iota(jnp.int32, (rows, rows), 1) // tok
    same_clip = row_clip == col_clip
    heads = [slice(start, start + HEAD_DIM) for start in range(0, query.shape[1], HEAD_DIM)]
    scores = [
        lax.dot_general(
            query[:, head], keys_ref[:, head], (((1,), (1,)), ((), ())), preferred_element_type=jnp.float32
        )
        for head in heads
    ]
    scores = [jnp.where(same_clip, score * (HEAD_DIM**-0.5), -jnp.inf) for score in scores]
    tops = [jnp.max(score, -1, keepdims=True) for score in scores]
    weights = [jnp.exp(score - top).astype(jnp.bfloat16) for score, top in zip(scores, tops)]
    ones = jnp.ones((rows, HEAD_DIM), jnp.bfloat16)
    sums = [jnp.dot(weight, ones, preferred_element_type=jnp.float32) for weight in weights]
    mixed = [
        jnp.dot(weight, values_ref[:, head], preferred_element_type=jnp.float32)
        for weight, head in zip(weights, heads)
    ]
    mixed = jnp.concatenate([(mix / total).astype(jnp.bfloat16) for mix, total in zip(mixed, sums)], 1)
    part = jnp.dot(mixed, wo_ref[...], preferred_element_type=jnp.float32)
    keep_ref[...] = part[:half]
    send_ref[...] = part[half:].astype(jnp.bfloat16)


def in_vmem(*arrays):
    return [pltpu.with_memory_space_constraint(a, pltpu.VMEM) for a in arrays]


def on_chip(kernel, outs, *arrays, flops=0):
    size = sum(a.size * a.dtype.itemsize for a in arrays)
    return pl.pallas_call(
        kernel,
        out_shape=tuple(jax.ShapeDtypeStruct(shape, dtype) for shape, dtype in outs),
        in_specs=[pl.BlockSpec(memory_space=pltpu.VMEM)] * len(arrays),
        out_specs=(pl.BlockSpec(memory_space=pltpu.VMEM),) * len(outs),
        cost_estimate=pl.CostEstimate(flops=flops, bytes_accessed=size, transcendentals=0),
        compiler_params=pltpu.CompilerParams(vmem_limit_bytes=16 << 20),
    )(*arrays)


def layer_part(own, partner, weights, tok, beside=()):
    wq, wkv, wo = weights[0], *in_vmem(weights[1]), weights[2]
    (half, width), head_cols = own.shape, wq.shape[1]
    partner_theirs = swapped(partner, 1)
    own_theirs = swapped(own, 1)
    if beside:
        partner_theirs, *beside = lax.optimization_barrier((partner_theirs, *beside))
    pushed = 2 * 256 * width * head_cols
    keys, values = on_chip(
        keyval_kernel,
        [((2 * half, head_cols), jnp.bfloat16)] * 2,
        partner, partner_theirs, wkv,
        flops=2 * pushed,
    )
    keep, send = on_chip(
        functools.partial(attend_kernel, tok),
        [((half, width), jnp.float32), ((half, width), jnp.bfloat16)],
        own, own_theirs, keys, values, wq, wo,
        flops=3 * pushed,
    )
    return keep, send, beside


def sum_kernel(state_ref, keep_ref, sent_ref, own_ref, *out_refs):
    tok = state_ref.shape[0]
    total = keep_ref[...] + sent_ref[...].astype(jnp.float32)
    own_ref[...] = state_ref[...].astype(jnp.float32) + total[-tok:]
    for k, out_ref in enumerate(out_refs, 1):
        start = total.shape[0] - (k + 1) * tok
        out_ref[...] = total[start : start + tok].astype(jnp.bfloat16)


def entry_kernel(x_ref, gain_ref, normed_ref, x_out, gain_out, sems):
    width = x_ref.shape[1] // PIECES
    copies = [pltpu.make_async_copy(gain_ref, gain_out, sems.at[PIECES])]
    for i in range(PIECES):
        here = (slice(None), pl.ds(i * width, width))
        copies.append(pltpu.make_async_copy(x_ref.at[here], x_out.at[here], sems.at[i]))
    for copy in copies:
        copy.start()
    for copy in copies:
        copy.wait()
    normed_ref[...] = normalized(x_out[...], gain_out[0])


def entry(state, gain):
    return pl.pallas_call(
        entry_kernel,
        out_shape=(
            pltpu.VMEM(state.shape, jnp.bfloat16),
            pltpu.VMEM(state.shape, state.dtype),
            pltpu.VMEM(gain.shape, gain.dtype),
        ),
        in_specs=[pl.BlockSpec(memory_space=pltpu.HBM)] * 2,
        out_specs=(pl.BlockSpec(memory_space=pltpu.VMEM),) * 3,
        scratch_shapes=[pltpu.SemaphoreType.DMA((PIECES + 1,))],
        compiler_params=pltpu.CompilerParams(vmem_limit_bytes=16 << 20),
    )(*in_hbm(state, gain))


def load_kernel(*refs):
    *refs, sems = refs
    count = len(refs) // 2
    copies = []
    for source, target in zip(refs[:count], refs[count:]):
        pieces = PIECES if source.shape[0] % (16 * PIECES) == 0 else 1
        rows = source.shape[0] // pieces
        for i in range(pieces):
            here = pl.ds(i * rows, rows)
            copies.append(pltpu.make_async_copy(source.at[here], target.at[here], sems.at[len(copies)]))
            copies[-1].start()
    for copy in copies:
        copy.wait()


def load(*arrays):
    return pl.pallas_call(
        load_kernel,
        out_shape=tuple(pltpu.VMEM(a.shape, a.dtype) for a in arrays),
        in_specs=[pl.BlockSpec(memory_space=pltpu.HBM)] * len(arrays),
        out_specs=(pl.BlockSpec(memory_space=pltpu.VMEM),) * len(arrays),
        scratch_shapes=[pltpu.SemaphoreType.DMA((PIECES * len(arrays),))],
        cost_estimate=pl.CostEstimate(
            flops=0, bytes_accessed=sum(a.size * a.dtype.itemsize for a in arrays), transcendentals=0
        ),
        compiler_params=pltpu.CompilerParams(vmem_limit_bytes=16 << 20),
    )(*in_hbm(*arrays))


def second_kernel(section_ref, lane_ref, offset_ref, fresh_ref, gain_ref, handed_ref, state_ref, normed_ref):
    tok = state_ref.shape[0]

    def block(index):
        return handed_ref[pl.ds(pl.multiple_of(index * tok, tok), tok)].astype(jnp.float32)

    odd = lane_ref[0] % 2
    count = handed_ref.shape[0] // (2 * tok)
    handed = 0.0
    for k in range(count):
        handed = handed + block((k + odd) % 2 * count + k)
    picked = fresh_ref[pl.ds(pl.multiple_of(offset_ref[0] * tok, tok), tok)]
    state = jnp.where(section_ref[0] == 0, picked, handed.astype(jnp.bfloat16))
    state_ref[...] = state
    normed_ref[...] = normalized(state, gain_ref[0])


def second_entry(section, lane, offsets, fresh, gain, handed, tok):
    shape = (tok, handed.shape[1])
    return pl.pallas_call(
        second_kernel,
        out_shape=(pltpu.VMEM(shape, jnp.bfloat16),) * 2,
        in_specs=[pl.BlockSpec(memory_space=pltpu.SMEM)] * 3 + [pl.BlockSpec(memory_space=pltpu.VMEM)] * 3,
        out_specs=(pl.BlockSpec(memory_space=pltpu.VMEM),) * 2,
        compiler_params=pltpu.CompilerParams(vmem_limit_bytes=16 << 20),
    )(section, lane, offsets, fresh, gain, handed)


def gathered(normed):
    lanes = lax.axis_size("lane")
    towers = [[tower * lanes + 2 * k for k in reversed(range(lanes // 2))] for tower in range(2)]
    partner = [swapped(normed, d) for d in towers[1]]
    own = [swapped(normed, d) if d else normed for d in towers[0]]
    return jnp.concatenate(own, 0), jnp.concatenate(partner, 0)


def summed(state, keep, send):
    shape = state.shape
    outs = [(shape, jnp.float32)] + [(shape, jnp.bfloat16)] * (keep.shape[0] // shape[0] - 1)
    own, *others = on_chip(sum_kernel, outs, *in_vmem(state), keep, swapped(send, 1))
    return own, others


def completed(own, others):
    for k, other in enumerate(others, 1):
        own = own + swapped(other, 2 * k).astype(jnp.float32)
    return own.astype(jnp.bfloat16)


def index_of(axis):
    return jnp.reshape(lax.axis_index(axis), (1,)).astype(jnp.int32)


def shards(in_flight, fresh_batches, offsets, norm_gain, w_query, w_keyval, w_out):
    normed, state, gain = entry(in_flight[0, 0], norm_gain[0])
    tok = state.shape[0]
    normed, section, lane = lax.optimization_barrier((normed, index_of("section"), index_of("lane")))
    (wkv,) = load(w_keyval.reshape(-1, w_keyval.shape[-1]))
    own, partner = gathered(normed)
    partner, wkv = lax.optimization_barrier((partner, wkv))
    wq, wo, fresh = w_query[0, 0], w_out[0, 0], fresh_batches.reshape(-1, fresh_batches.shape[-1])
    weights = (wq, wkv, wo)
    first_sum, others = summed(state, *layer_part(own, partner, weights, tok)[:2])
    handed = handed_on(first_sum.astype(jnp.bfloat16), others)
    state, normed = second_entry(section, lane, offsets, fresh, gain, handed, tok)
    normed, others = lax.optimization_barrier((normed, others))
    own, partner = gathered(normed)
    arrived = [swapped(other, 2 * k) for k, other in enumerate(others, 1)]
    keep, send, arrived = layer_part(own, partner, weights, tok, arrived)
    first = sum([rows.astype(jnp.float32) for rows in arrived], first_sum).astype(jnp.bfloat16)
    second = completed(*summed(state, keep, send))
    return jnp.stack([first, second])[:, None, None]


def solution(mesh):
    placed = (
        P("section", "tower", "lane", None),
        P(None, "tower", "lane", None),
        P("lane"),
        P("section", "tower", None),
        P("section", "tower", None, "lane"),
        P("section", "tower", None, None, "lane"),
        P("section", "tower", "lane", None),
    )
    return jax.shard_map(
        shards,
        mesh=mesh,
        in_specs=placed,
        out_specs=P(None, "section", "tower", "lane", None),
        check_vma=False,
    )
```
